128 devices in a mesh: dp: 32 (over x, y, z_lo), tensor: 4 (over z_hi, core).
Axes of the slice: x: 4, y: 4, z: 4 (z_hi: 2, z_lo: 2; z = z_hi * 2 + z_lo), core: 2. Of those that a mesh axis runs over, the one named last changes fastest.
Arguments:
- hidden_in: bfloat16 [32768, 1536], P(('dp', 'tensor')), may hold values from -6 to 6
- norm_gain: bfloat16 [1536], replicated, may hold values from 0.5 to 1.5
- w_z: bfloat16 [1536, 3072], P('dp', 'tensor'), may hold values from -0.15625 to 0.15625
- w_x: bfloat16 [1536, 3072], P('dp', 'tensor'), may hold values from -0.15625 to 0.15625
- w_bc: bfloat16 [1536, 256], P('dp'), may hold values from -0.15625 to 0.15625
- w_dt: bfloat16 [1536, 48], P('dp', 'tensor'), may hold values from -0.15625 to 0.15625
- conv_x: bfloat16 [4, 3072], P(None, 'tensor'), may hold values from -3 to 3
- conv_x_bias: bfloat16 [3072], P('tensor'), may hold values from -3 to 3
- conv_bc: bfloat16 [4, 256], replicated, may hold values from -3 to 3
- conv_bc_bias: bfloat16 [256], replicated, may hold values from -3 to 3
- dt_bias: float32 [48], P('tensor'), may hold values from -6 to -1.5
- a_log: float32 [48], P('tensor'), may hold values from -3 to 1
- skip_d: float32 [48], P('tensor'), may hold values from 0.5 to 1.5
- gate_norm: bfloat16 [3072], P('tensor'), may hold values from 0.5 to 1.5
- w_out: bfloat16 [3072, 1536], P('tensor', 'dp'), may hold values from -0.109375 to 0.109375
- lengths: int32 [32, 4], P('dp'), may hold values from 0 to 1024, as said below
- out_grad: bfloat16 [32768, 1536], P(('dp', 'tensor')), may hold values from -24 to 24
Outputs:
- block_out: float32 [32768, 1536], P(('dp', 'tensor'))
- input_grad: float32 [32768, 1536], P(('dp', 'tensor'))
- norm_gain_grad: float32 [1536], replicated
- w_z_grad: float32 [1536, 3072], P('dp', 'tensor')
- w_x_grad: float32 [1536, 3072], P('dp', 'tensor')
- w_bc_grad: float32 [1536, 256], P('dp')
- w_dt_grad: float32 [1536, 48], P('dp', 'tensor')
- conv_x_grad: float32 [4, 3072], P(None, 'tensor')
- conv_x_bias_grad: float32 [3072], P('tensor')
- conv_bc_grad: float32 [4, 256], replicated
- conv_bc_bias_grad: float32 [256], replicated
- dt_bias_grad: float32 [48], P('tensor')
- a_log_grad: float32 [48], P('tensor')
- skip_d_grad: float32 [48], P('tensor')
- gate_norm_grad: float32 [3072], P('tensor')
- w_out_grad: float32 [3072, 1536], P('tensor', 'dp')
The draws below stay inside these ranges and needn't reach their ends.
Inputs may be any that keep to these rules, and one draw needn't show every extreme that they name: Each group's lengths sum to 1024 or less; one of them is 770 or more and starts within the group's first 256 rows; in every draw some group is one sequence of exactly 1024; lengths of 0 occur.
All inputs are finite; a program needn't handle non-finite values.
Results may differ from the reference program's by a relative error of at most 0.011.
Values may be sent and summed in bfloat16 or wider, within the bound.
A program may use at most 128 MiB of HBM per device.

```python
import jax
import jax.numpy as jnp
from jax import lax

D = 1536
HEADS = 48
HEAD_DIM = 64
STATE = 128
KERNEL = 4
STRETCH = 256
SEQS = 4
INNER = 3072
GROUP = 1024
ROWS = 32768
N_DP = 32


def draw_lengths(key, part):
    key = jax.random.fold_in(key, 11)
    keys = jax.random.split(key, 5)
    longest = jax.random.randint(keys[0], (N_DP,), 3 * GROUP // 4 + 2, GROUP + 1)
    forced = jax.random.randint(keys[1], (), 0, N_DP)
    longest = jnp.where(jnp.arange(N_DP) == forced, GROUP, longest).astype(jnp.int32)
    remain = GROUP - longest
    padding = jax.random.randint(keys[2], (N_DP,), 0, remain + 1)
    short_total = remain - padding
    cuts = jax.random.randint(keys[3], (N_DP, SEQS - 2), 0, short_total[:, None] + 1)
    cuts = jnp.sort(cuts, axis=1)
    edges = jnp.concatenate([jnp.zeros((N_DP, 1), jnp.int32), cuts.astype(jnp.int32), short_total[:, None].astype(jnp.int32)], axis=1)
    shorts = edges[:, 1:] - edges[:, :-1]
    slot_of_long = jax.random.randint(keys[4], (N_DP,), 0, SEQS)
    slot_index = jnp.arange(SEQS, dtype=jnp.int32)[None, :]
    source = slot_index - (slot_index > slot_of_long[:, None]).astype(jnp.int32)
    source = jnp.clip(source, 0, SEQS - 2)
    placed = jnp.take_along_axis(shorts, source, axis=1)
    return jnp.where(slot_index == slot_of_long[:, None], longest[:, None], placed).astype(jnp.int32)


def raised(entries, stream_key, source, target, blocks, factor):
    owner, partner = [(jnp.arange(entries.shape[position]) // (entries.shape[position] // blocks)).reshape([-1 if axis == position else 1 for axis in range(entries.ndim)]) for position in (source, target)]
    chosen = jax.random.permutation(stream_key, blocks)[partner]
    strong = (owner == chosen) | (owner == (partner + blocks // 2) % blocks)
    return jnp.where(strong, factor * entries, entries)


def shard_levels(rng, dims, cuts, smallest, largest):
    level, own = 1.0, jax.random.fold_in(rng, 6)
    for position, parts in cuts:
        heights = jnp.exp(jax.random.uniform(jax.random.fold_in(own, position), (parts,), jnp.float32, smallest / len(cuts), largest / len(cuts)))
        level = level * jnp.repeat(heights, dims[position] // parts).reshape([-1 if axis == position else 1 for axis in range(len(dims))])
    return level


def noise(key, extent, deviation, limit, cuts=(), kind=jnp.bfloat16):
    array = deviation * jax.random.normal(key, extent, jnp.float32)
    if cuts:
        array = array * shard_levels(key, extent, cuts, -0.22, 0.18)
    return jnp.clip(array, -limit, limit).astype(kind)


def noise_with(stream_key, shape, scale, reach, shards, heavy, held_as=jnp.bfloat16):
    values = scale * jax.random.normal(stream_key, shape, jnp.float32)
    if shards:
        values = values * shard_levels(stream_key, shape, shards, -0.22, 0.18)
    return jnp.clip(raised(values, jax.random.fold_in(stream_key, 3), *heavy), -reach, reach).astype(held_as)


def setup_inputs(seed: int = 0) -> dict:
    arg_keys = jax.random.split(jax.random.key(seed), 18)
    return {
        "hidden_in": noise(arg_keys[0], (ROWS, D), 1.0, 6.0, ((0, 128),)),
        "norm_gain": jnp.clip(1.0 + 0.1 * jax.random.normal(arg_keys[1], (D,), jnp.float32), 0.5, 1.5).astype(jnp.bfloat16),
        "w_z": noise(arg_keys[2], (D, INNER), D ** -0.5, 0.15625, ((0, 32), (1, 4))),
        "w_x": noise(arg_keys[3], (D, INNER), D ** -0.5, 0.15625, ((0, 32), (1, 4))),
        "w_bc": noise(arg_keys[4], (D, 2 * STATE), D ** -0.5, 0.15625, ((0, 32),)),
        "w_dt": noise(arg_keys[5], (D, HEADS), D ** -0.5, 0.15625, ((0, 32), (1, 4))),
        "conv_x": noise(arg_keys[6], (KERNEL, INNER), KERNEL ** -0.5, 3.0, ((1, 4),)),
        "conv_x_bias": noise(arg_keys[7], (INNER,), 0.5, 3.0, ((0, 4),)),
        "conv_bc": noise(arg_keys[8], (KERNEL, 2 * STATE), KERNEL ** -0.5, 3.0),
        "conv_bc_bias": noise(arg_keys[9], (2 * STATE,), 0.5, 3.0),
        "dt_bias": jnp.clip(-6.0 + 4.5 * jax.random.uniform(arg_keys[10], (HEADS,), jnp.float32) ** shard_levels(arg_keys[10], (HEADS,), ((0, 4),), -0.2, 0.2), -6.0, -1.5),
        "a_log": jnp.clip(-3.0 + 4.0 * jax.random.uniform(arg_keys[11], (HEADS,), jnp.float32) ** shard_levels(arg_keys[11], (HEADS,), ((0, 4),), -0.2, 0.2), -3.0, 1.0),
        "skip_d": jnp.clip(0.5 + 1.0 * jax.random.uniform(arg_keys[12], (HEADS,), jnp.float32) ** shard_levels(arg_keys[12], (HEADS,), ((0, 4),), -0.2, 0.2), 0.5, 1.5),
        "gate_norm": jnp.clip(1.0 + 0.1 * jax.random.normal(arg_keys[13], (INNER,), jnp.float32), 0.5, 1.5).astype(jnp.bfloat16),
        "w_out": noise(arg_keys[14], (INNER, D), INNER ** -0.5, 0.109375, ((0, 4), (1, 32))),
        "lengths": draw_lengths(jax.random.fold_in(arg_keys[17], 71), 0),
        "out_grad": noise_with(arg_keys[16], (ROWS, D), 1.0, 24.0, ((0, 128),), (0, 1, 128, 5.5)),
    }


@jax.custom_vjp
def low(v):
    return lax.optimization_barrier(v.astype(jnp.bfloat16)).astype(jnp.float32)

@jax.custom_vjp
def low_back(v):
    return v

def low_keep(v):
    return (low(v), None)

def low_pass(kept, grad):
    return (grad,)

def back_keep(v):
    return (v, None)

def back_low(kept, grad):
    return (low(grad),)
low.defvjp(low_keep, low_pass)
low_back.defvjp(back_keep, back_low)
highest = lax.Precision.HIGHEST
epsilon = 1e-05

def matmul_high(left, right):
    return jnp.dot(left, right, precision=highest, preferred_element_type=jnp.float32)

def silu_of(values):
    return values * jax.nn.sigmoid(values)

def segment_ids(lengths_row, total_rows):
    seq_ends = jnp.cumsum(lengths_row).astype(jnp.int32)
    places = jnp.arange(total_rows, dtype=jnp.int32)
    seg_ids = lax.optimization_barrier(jnp.sum((places[:, None] >= seq_ends[None, :]).astype(jnp.int32), axis=1)).astype(jnp.int32)
    alive = (places < seq_ends[-1]).astype(jnp.float32)
    return (seg_ids, alive)

def causal_conv(values, kernel, kernel_bias, seg_ids):
    total_rows = values.shape[0]
    summed = kernel_bias[None, :] + kernel[KERNEL - 1][None, :] * values
    for offset in range(1, KERNEL):
        moved = jnp.concatenate([jnp.zeros((offset, values.shape[1]), jnp.float32), values[:total_rows - offset]], axis=0)
        moved_ids = jnp.concatenate([jnp.full((offset,), -1, jnp.int32), seg_ids[:total_rows - offset]])
        same_seq = (moved_ids == seg_ids).astype(jnp.float32)
        summed = summed + kernel[KERNEL - 1 - offset][None, :] * moved * same_seq[:, None]
    return silu_of(summed)

def state_scan(values, steps, b_proj, c_proj, seg_ids, rates):
    total_rows, heads, width = values.shape
    blocks = total_rows // STRETCH
    block_values = values.reshape(blocks, STRETCH, heads, width)
    block_steps = steps.reshape(blocks, STRETCH, heads)
    block_b = b_proj.reshape(blocks, STRETCH, STATE)
    block_c = c_proj.reshape(blocks, STRETCH, STATE)
    block_ids = seg_ids.reshape(blocks, STRETCH)
    earlier = jnp.concatenate([jnp.full((1,), -1, jnp.int32), block_ids[:-1, STRETCH - 1]])
    positions = jnp.arange(STRETCH, dtype=jnp.int32)
    causal = positions[:, None] >= positions[None, :]

    def advance(carried, pieces):
        part_values, part_steps, part_b, part_c, part_ids, before_id = pieces
        log_decay = jnp.cumsum(part_steps * rates[None, :], axis=0)
        same_seq = (part_ids[:, None] == part_ids[None, :]) & causal
        spans = log_decay[:, None, :] - log_decay[None, :, :]
        decays = jnp.exp(jnp.where(same_seq[:, :, None], spans, -jnp.inf))
        scores = lax.dot_general(part_c, part_b, (((1,), (1,)), ((), ())), precision=highest, preferred_element_type=jnp.float32)
        mixing = scores[:, :, None] * decays * part_steps[None, :, :]
        result = jnp.einsum('tsh,shp->thp', mixing, part_values, precision=highest)
        inherit = (part_ids == before_id).astype(jnp.float32)
        readout = jnp.einsum('tn,hpn->thp', part_c, carried, precision=highest)
        result = result + jnp.exp(log_decay)[:, :, None] * inherit[:, None, None] * readout
        last_id = part_ids[STRETCH - 1]
        tail_same = (part_ids == last_id).astype(jnp.float32)
        towards = jnp.exp(log_decay[STRETCH - 1][None, :] - log_decay) * tail_same[:, None] * part_steps
        fresh = jnp.einsum('shp,sn->hpn', towards[:, :, None] * part_values, part_b, precision=highest)
        keep_state = (last_id == before_id).astype(jnp.float32)
        carried = keep_state * jnp.exp(log_decay[STRETCH - 1])[:, None, None] * carried + fresh
        return (carried, result)
    initial = jnp.zeros((heads, width, STATE), jnp.float32)
    leftover, outputs = lax.scan(jax.checkpoint(advance), initial, (block_values, block_steps, block_b, block_c, block_ids, earlier))
    return outputs.reshape(total_rows, heads, width)

def mixer(seg_ids, inner_x, inner_bc, step_raw, kernel_x, bias_x, kernel_bc, bias_bc, step_bias, log_rate, skip_gain):
    conv_out = causal_conv(inner_x, kernel_x, bias_x, seg_ids)
    bc_out = causal_conv(inner_bc, kernel_bc, bias_bc, seg_ids)
    step_sizes = jax.nn.softplus(step_raw + step_bias[None, :])
    rates = -jnp.exp(log_rate)
    total_rows = inner_x.shape[0]
    heads = step_bias.shape[0]
    values = conv_out.reshape(total_rows, heads, HEAD_DIM)
    result = state_scan(values, step_sizes, bc_out[:, :STATE], bc_out[:, STATE:], seg_ids, rates) + skip_gain[None, :, None] * values
    return result.reshape(total_rows, heads * HEAD_DIM)

def group_forward(params, hidden, seg_ids, alive):
    gain_vec, wz_full, wx_full, wbc_full, wdt_full, kernel_x, bias_x, kernel_bc, bias_bc, step_bias, log_rate, skip_gain, gnorm_vec, wout_full = params
    inv_rms = lax.rsqrt(lax.optimization_barrier(jnp.mean(hidden * hidden, axis=-1)) + epsilon)
    normed = low(hidden * inv_rms[:, None] * gain_vec[None, :])
    gate_pre = low_back(matmul_high(normed, wz_full))
    inner_x = low_back(matmul_high(normed, wx_full))
    inner_bc = low_back(matmul_high(normed, wbc_full))
    step_raw = low_back(matmul_high(normed, wdt_full))
    mixed = mixer(seg_ids, inner_x, inner_bc, step_raw, kernel_x, bias_x, kernel_bc, bias_bc, step_bias, log_rate, skip_gain)
    gated = mixed * silu_of(gate_pre)
    inv_gated = lax.rsqrt(lax.optimization_barrier(jnp.mean(gated * gated, axis=-1)) + epsilon)
    normed_out = low(gated * inv_gated[:, None] * gnorm_vec[None, :])
    return hidden + alive[:, None] * matmul_high(normed_out, wout_full)

def reference(hidden_in, norm_gain, w_z, w_x, w_bc, w_dt, conv_x, conv_x_bias, conv_bc, conv_bc_bias, dt_bias, a_log, skip_d, gate_norm, w_out, lengths, out_grad):
    params = (norm_gain.astype(jnp.float32), w_z.astype(jnp.float32), w_x.astype(jnp.float32), w_bc.astype(jnp.float32), w_dt.astype(jnp.float32), conv_x.astype(jnp.float32), conv_x_bias.astype(jnp.float32), conv_bc.astype(jnp.float32), conv_bc_bias.astype(jnp.float32), dt_bias.astype(jnp.float32), a_log.astype(jnp.float32), skip_d.astype(jnp.float32), gate_norm.astype(jnp.float32), w_out.astype(jnp.float32))
    grouped_in = hidden_in.astype(jnp.float32).reshape(N_DP, GROUP, D)
    grouped_cot = out_grad.astype(jnp.float32).reshape(N_DP, GROUP, D)

    def one_group(totals, pieces):
        hidden, cotangent, lengths_row = pieces
        seg_ids, alive = segment_ids(lengths_row, GROUP)

        def forward_fn(param_set, hidden_rows):
            return group_forward(param_set, hidden_rows, seg_ids, alive)
        output, pullback = jax.vjp(forward_fn, params, hidden)
        grad_params, grad_hidden = pullback(cotangent)
        totals = jax.tree.map(lambda first, second: first + second, totals, grad_params)
        return (totals, (output, grad_hidden))
    zero_grads = jax.tree.map(jnp.zeros_like, params)
    grads, (outputs, hidden_grads) = lax.scan(one_group, zero_grads, (grouped_in, grouped_cot, lengths))
    return (outputs.reshape(ROWS, D), hidden_grads.reshape(ROWS, D), grads[0], grads[1], grads[2], grads[3], grads[4], grads[5], grads[6], grads[7], grads[8], grads[9], grads[10], grads[11], grads[12], grads[13])
```

```python
import jax
import jax.numpy as jnp
from jax import lax
from jax.experimental import pallas as pl
from jax.experimental.pallas import tpu as pltpu
from jax.sharding import PartitionSpec as P

f32=jnp.float32; bf16=jnp.bfloat16
T=1024; L=256; NC=4; D=1536; W=768; NP=6; N=128; HALO=8
HI=lax.Precision.HIGHEST
NEG=-1e30

def nn(a,b,prec=None): return lax.dot_general(a,b,(((1,),(0,)),((),())),precision=prec,preferred_element_type=f32)
def nt(a,b,prec=None): return lax.dot_general(a,b,(((1,),(1,)),((),())),precision=prec,preferred_element_type=f32)
def tn(a,b,prec=None): return lax.dot_general(a,b,(((0,),(0,)),((),())),precision=prec,preferred_element_type=f32)

def iota(shape,d): return lax.broadcasted_iota(jnp.int32,shape,d)
def seg_of(idx,ends):
    s=(idx>=ends[0]).astype(jnp.int32)
    for k in range(1,4): s=s+(idx>=ends[k]).astype(jnp.int32)
    return s
def sig(v): return 0.5*jnp.tanh(0.5*v)+0.5
def softplus(v): return jnp.maximum(v,0.0)+jnp.log1p(jnp.exp(-jnp.abs(v)))

def chunk_masks(ends,r0):
    ri=iota((L,128),0)+r0
    sg=seg_of(ri,ends)
    return sg,[None]+[(seg_of(ri-j,ends)==sg) for j in (1,2,3)]
def pair_cols(a,j,lo):
    return jnp.where(lo,a[:,2*j:2*j+1],a[:,2*j+1:2*j+2])
def taps(w,masks,halo):
    out=[w[halo:halo+L]]
    for q in (1,2,3):
        out.append(jnp.where(masks[q],w[halo-q:halo-q+L],0.0))
    return out
def conv_pre(ws,pv,kcols):
    s=pv[4:5,kcols]+pv[3:4,kcols]*ws[0]
    for q in (1,2,3): s=s+pv[3-q:4-q,kcols]*ws[q]
    return s

def head_steps(sraw,hv):
    dtp=sraw+hv[0:1,:]
    dt=softplus(dtp)
    return dtp,dt
def chunk_decay(ends,r0,dt,hv,ltri):
    dA=dt*hv[1:2,:]
    cs=nn(ltri,dA,HI)
    return dA,cs
def seg_scalars(ends,r0):
    before=seg_of(r0-1,ends); last=seg_of(r0+L-1,ends)
    return before,last
def chunk_state_decays(cs,sg,before,last):
    e=jnp.where(sg==before,jnp.exp(cs),0.0)
    csl=cs[L-1:L,:]
    w=jnp.where(sg==last,jnp.exp(csl-cs),0.0)
    kd=jnp.exp(csl)*jnp.where(before==last,1.0,0.0)
    return e,w,kd

def fwd_chunk(c,ends,nx,wa,pv,pb,hv,ix16,ixh,tmp,ibc,sraw,pre,mixed,yi,sin,bc16,S):
    r0=pl.multiple_of(c*L,L); rp=pl.multiple_of(c*L+HALO,8)
    rows=pl.ds(r0,L); rows_p=pl.ds(rp,L)
    n=nx[c]
    t=nn(n,wa[:,:,:,0:W].reshape(D,W))
    tmp[...]=t
    ix16[pl.ds(pl.multiple_of(c*L+16,16),L),:]=t.astype(bf16)
    t=nn(n,wa[:,:,:,W:].reshape(D,384))
    ibc[rows_p,:]=t[:,:256]
    sraw[rows,:]=t[:,256:]
    lane=iota((L,128),1); lo=lane<64
    sg,masks=chunk_masks(ends,r0)
    ti=iota((L,L),0); si=iota((L,L),1)
    mask=(seg_of(ti+r0,ends)==seg_of(si+r0,ends))&(ti>=si)
    ltri=(ti>=si).astype(f32)
    dtp,dt=head_steps(sraw[rows,:],hv)
    dA,cs=chunk_decay(ends,r0,dt,hv,ltri)
    csT=cs.T
    before,last=seg_scalars(ends,r0)
    e,w,kd=chunk_state_decays(cs,sg,before,last)
    win=pl.ds(r0,L+HALO)
    bc=[]
    for k in range(2):
        cols=slice(128*k,128*k+128)
        p=conv_pre(taps(ibc[win,cols],masks,HALO),pb,cols)
        v=(p*sig(p)).astype(bf16)
        bc16[rows,cols]=v
        bc.append(v)
    B,C=bc
    BT=B.T
    sc=nt(C,B)
    for j in range(NP):
        cols=slice(128*j,128*j+128)
        p=conv_pre(taps(jnp.concatenate([ixh[:,cols],tmp[:,cols]],axis=0),masks,HALO),pv,cols)
        ixh[:,cols]=tmp[L-HALO:L,cols]
        pre[rows,cols]=p
        xc=p*sig(p)
        u=pair_cols(dt,j,lo)*xc
        ub=u.astype(bf16)
        y=None
        for q in range(2):
            h=2*j+q
            dec=jnp.exp(jnp.where(mask,cs[:,h:h+1]-csT[h:h+1,:],NEG))
            M=(sc*dec).astype(bf16)
            uq=jnp.where(lo if q==0 else ~lo,ub,jnp.zeros_like(ub))
            t=nn(M,uq)
            y=t if y is None else y+t
        yi[rows,cols]=y
        Sj=S[:,cols]
        Sb=Sj.astype(bf16)
        sin[c,:,cols]=Sb
        y=y+pair_cols(e,j,lo)*nn(C,Sb)
        mixed[rows,cols]=y+pv[6:7,cols]*xc
        uw=(u*pair_cols(w,j,lo)).astype(bf16)
        S[:,cols]=pair_cols(kd,j,lo[:1])*Sj+nn(BT,uw)

def bwd_chunk(c,ends,pv,pb,hv,ix16,ibc,sraw,pre,mixed,yi,sin,bc16,gm,dS,
              q1,q3,dpre,rx,dbc,rstep,dk,hs):
    r0=pl.multiple_of(c*L,L)
    rows=pl.ds(r0,L)
    lane=iota((L,128),1); lo=lane<64
    sg,masks=chunk_masks(ends,r0)
    ri=iota((L,128),0)+r0
    up=[None]+[((seg_of(ri+j,ends)==sg)&(ri+j<T)) for j in (1,2,3)]
    ti=iota((L,L),0); si=iota((L,L),1)
    maskT=(seg_of(ti+r0,ends)==seg_of(si+r0,ends))&(si>=ti)
    ltri=(ti>=si).astype(f32)
    dtp,dt=head_steps(sraw[rows,:],hv)
    dA,cs=chunk_decay(ends,r0,dt,hv,ltri)
    csT=cs.T
    before,last=seg_scalars(ends,r0)
    e,w,kd=chunk_state_decays(cs,sg,before,last)
    B=bc16[rows,0:128]; C=bc16[rows,128:256]
    CT=C.T
    scT=nt(B,C)
    acc=jnp.zeros((L,L),f32); dCin=jnp.zeros((L,N),f32); dBout=jnp.zeros((L,N),f32)
    win=pl.ds(r0,L+16)
    rowq=[]
    for j in range(NP):
        cols=slice(128*j,128*j+128)
        g=gm[rows,cols]; gb=g.astype(bf16)
        p=pre[rows,cols]; s=sig(p); xc=p*s
        dtx=pair_cols(dt,j,lo)
        u=dtx*xc; ub=u.astype(bf16)
        sk=pv[6:7,cols]
        du=None
        for q in range(2):
            h=2*j+q
            dec=jnp.exp(jnp.where(maskT,csT[h:h+1,:]-cs[:,h:h+1],NEG))
            M=(scT*dec).astype(bf16)
            gq=jnp.where(lo if q==0 else ~lo,gb,jnp.zeros_like(gb))
            t=nn(M,gq)
            du=t if du is None else du+t
            acc=acc+nt(ub,gq)*dec
        dSj=dS[:,cols]; dSb=dSj.astype(bf16)
        Sb=sin[c,:,cols]
        wx_=pair_cols(w,j,lo); ex=pair_cols(e,j,lo)
        duo=wx_*nn(B,dSb)
        gef=g*ex
        ge=gef.astype(bf16); uw=(u*wx_).astype(bf16)
        dCin=dCin+nt(ge,Sb)
        dBout=dBout+nt(uw,dSb)
        yij=yi[rows,cols]
        y_in=mixed[rows,cols]-yij-sk*xc
        udo=u*duo
        q1[:,cols]=(gb.astype(f32)*yij-ub.astype(f32)*du)+(g*y_in-udo)
        du=du+duo
        q3[:,cols]=xc*du
        kdj=pair_cols(kd,j,lo[:1])
        rowq.append(jnp.sum(udo,0,keepdims=True)+jnp.sum(kdj*Sb.astype(f32)*dSj,0,keepdims=True))
        dS[:,cols]=kdj*dSj+nn(CT,ge)
        dxc=dtx*du+sk*g
        dp=dxc*(s*(1.0+p*(1.0-s)))
        ws=taps(ix16[win,cols].astype(f32),masks,16)
        dk[4:5,cols]+=jnp.sum(dp,0,keepdims=True)
        dk[5:6,cols]+=jnp.sum(g*xc,0,keepdims=True)
        for t_ in range(4):
            dk[3-t_:4-t_,cols]+=jnp.sum(dp*ws[t_],0,keepdims=True)
        wd=jnp.concatenate([dp,dpre[:,cols]],axis=0)
        dpre[:,cols]=dp[0:HALO]
        dv=pv[3:4,cols]*dp
        for t_ in (1,2,3):
            dv=dv+pv[3-t_:4-t_,cols]*jnp.where(up[t_],wd[t_:t_+L],0.0)
        rx[c,:,cols]=dv.astype(bf16)
    ab=acc.astype(bf16)
    dbc[:,0:128]=nn(ab,C)+dBout
    dbc[:,128:256]=nn(ab.T,B)+dCin
    he=((iota((W,128),0)//64)==iota((W,128),1)).astype(f32)
    dcs=nn(q1[...],he,HI)
    tailv=nn(jnp.broadcast_to(jnp.concatenate(rowq,axis=1),(8,W)),he,HI)[0:1,:]
    dcs=dcs+jnp.where(iota((L,128),0)==L-1,tailv,0.0)
    ddA=nn((si>=ti).astype(f32),dcs,HI)
    ddt=nn(q3[...],he,HI)+hv[1:2,:]*ddA
    hs[1:2,:]+=jnp.sum(ddA*dA,0,keepdims=True)
    dsr=ddt*sig(dtp)
    hs[0:1,:]+=jnp.sum(dsr,0,keepdims=True)
    rstep[c]=dsr.astype(bf16)
MESH = pl.DeviceIdType.MESH


def position():
    d = lax.axis_index("dp")
    t = lax.axis_index("tensor")
    return d // 8, (d // 2) % 4, d % 2, t // 2, t % 2


def device(x, y, zl, zh, c):
    return (lax.rem(x, 4) * 8 + lax.rem(y, 4) * 2 + zl, zh * 2 + c)


class Peers:
    def __init__(self):
        self.x, self.y, self.zl, self.zh, self.c = x, y, zl, zh, c = position()
        self.along_x = [device(x + k, y, zl, zh, c) for k in (1, 2, 3)]
        self.along_y = [device(x, y + k, zl, zh, c) for k in (1, 2, 3)]
        self.pair = device(x, y, 1 - zl, zh, c)
        self.far = device(x, y, zl, 1 - zh, c)
        self.near = device(x, y, zl, zh, 1 - c)
        self.cross = device(x, y, zl, 1 - zh, 1 - c)
        self.rank = zh * 2 + c
        self.group = [self.near, self.far, self.cross]
        self.all = self.along_x + self.along_y + [self.pair, self.far, self.near, self.cross]


def greet(devices):
    barrier = pltpu.get_barrier_semaphore()
    for other in devices:
        pl.semaphore_signal(barrier, inc=1, device_id=other, device_id_type=MESH)
    pl.semaphore_wait(barrier, len(devices))


def remote(src, dst, sems, k, to):
    return pltpu.make_async_remote_copy(
        src_ref=src, dst_ref=dst, send_sem=sems.at[0, k], recv_sem=sems.at[1, k], device_id=to, device_id_type=MESH
    )


def start_all(copies):
    for copy in copies:
        copy.start()


def wait_all(copies):
    for copy in copies:
        copy.wait()


class Ring:
    def __init__(self, at, mine, line, sems, first):
        plus, minus = line[0], line[2]
        before, after = lax.rem(mine + 3, 4), lax.rem(mine + 1, 4)
        own = [at(mine, 0), at(mine, 1)]
        self.own = [
            remote(own[0], own[0], sems, first, plus),
            remote(own[1], own[1], sems, first + 1, minus),
            remote(own[1], own[1], sems, first + 2, plus),
            remote(own[0], own[0], sems, first + 3, minus),
        ]
        self.onward = [
            remote(at(before, 0), at(before, 0), sems, first + 4, plus),
            remote(at(after, 1), at(after, 1), sems, first + 5, minus),
        ]

    def start(self):
        start_all(self.own)

    def forward(self):
        for k in range(2):
            self.own[k].wait()
            self.onward[k].start()

    def finish(self):
        wait_all(self.own[2:])
        wait_all(self.onward)


class WeightGather:
    def __init__(self, pieces, full, split, sems, p):
        x, y = p.x, p.y
        cols = full.shape[3]
        a, b = pl.ds(0, split), pl.ds(split, cols - split)
        mine = pl.ds(pl.multiple_of(p.zl * 48, 16), 48)
        self.mine = mine
        self.z = remote(full.at[x, y, mine, :], full.at[x, y, mine, :], sems, 0, p.pair)
        self.own = [
            pltpu.make_async_copy(piece, full.at[x, y, mine, pl.ds(at, width)], sems.at[0, 19 + k])
            for k, (piece, at, width) in enumerate(pieces)
        ]
        self.mid = []
        for k in range(3):
            ya, xb = full.at[x, y, :, a], full.at[x, y, :, b]
            self.mid.append(remote(ya, ya, sems, 1 + k, p.along_y[k]))
            self.mid.append(remote(xb, xb, sems, 4 + k, p.along_x[k]))
        self.last = [
            Ring(lambda o, h: full.at[o, pl.ds(2 * h, 2), :, a], x, p.along_x, sems, 7),
            Ring(lambda o, h: full.at[pl.ds(2 * h, 2), o, :, b], y, p.along_y, sems, 13),
        ]

    def load(self):
        start_all(self.own)

    def first(self):
        wait_all(self.own)
        self.z.start()

    def second(self):
        self.z.wait()
        start_all(self.mid)

    def third(self):
        wait_all(self.mid)
        start_all(self.last)

    def forward(self):
        for ring in self.last:
            ring.forward()

    def finish(self):
        for ring in self.last:
            ring.finish()


class WeightScatter:
    def __init__(self, part, got1, got2, got3, split, sems, p):
        x, y = p.x, p.y
        cols = got3.shape[1]
        self.part, self.got1, self.got2, self.got3, self.p = part, got1, got2, got3, p
        self.a, self.b = a, b = pl.ds(0, split), pl.ds(split, cols - split)
        mine = pl.ds(pl.multiple_of(p.zl * 48, 16), 48)
        other = pl.ds(pl.multiple_of((1 - p.zl) * 48, 16), 48)
        self.mine = mine
        self.one = []
        self.two = []
        for k in range(3):
            xk, yk = lax.rem(x + k + 1, 4), lax.rem(y + k + 1, 4)
            self.one.append(remote(part.at[xk, :, :, a], got1.at[k, :, :, a], sems, k, p.along_x[k]))
            if b.size:
                self.one.append(remote(part.at[:, yk, :, b], got1.at[k, :, :, b], sems, 3 + k, p.along_y[k]))
            self.two.append(remote(part.at[x, yk, :, a], got2.at[k, :, a], sems, 6 + k, p.along_y[k]))
            if b.size:
                self.two.append(remote(part.at[xk, y, :, b], got2.at[k, :, b], sems, 9 + k, p.along_x[k]))
        self.three = remote(part.at[x, y, other, :], got3, sems, 12, p.pair)

    def first(self):
        start_all(self.one)

    def second(self):
        wait_all(self.one)
        x, y, part, got = self.p.x, self.p.y, self.part, self.got1

        @pl.loop(0, 4)
        def _(i):
            for cut, at in ((self.a, (x, i)), (self.b, (i, y))):
                if cut.size:
                    total = part[at[0], at[1], :, cut].astype(f32)
                    for k in range(3):
                        total = total + got[k, i, :, cut].astype(f32)
                    part[at[0], at[1], :, cut] = total.astype(bf16)

        start_all(self.two)

    def third(self):
        wait_all(self.two)
        total = self.part[self.p.x, self.p.y].astype(f32)
        for k in range(3):
            total = total + self.got2[k].astype(f32)
        self.part[self.p.x, self.p.y] = total.astype(bf16)
        self.three.start()

    def finish(self):
        self.three.wait()
        return self.part[self.p.x, self.p.y, self.mine, :].astype(f32) + self.got3[...].astype(f32)


class RowGather:
    def __init__(self, own, full, sems, p):
        me, across = p.rank, (1 - p.zh) * 2 + p.c
        self.to_far = remote(own, full.at[me], sems, 0, p.far)
        self.to_near = remote(own, full.at[me], sems, 1, p.near)
        self.onward = remote(full.at[across], full.at[across], sems, 2, p.near)
        self.own = pltpu.make_async_copy(own, full.at[me], sems.at[0, 3])

    def first(self):
        self.to_far.start()
        self.to_near.start()
        self.own.start()

    def forward(self):
        self.to_far.wait()
        self.onward.start()

    def finish(self):
        self.onward.wait()


class RowScatter:
    def __init__(self, part, near, far, sems, p):
        self.part, self.near, self.far, self.p = part, near, far, p
        self.copies = [
            remote(part.at[z * 2 + 1 - p.c], near.at[k], sems, k, p.near)
            for k, z in ((0, 1 - p.zh), (1, p.zh))
        ]
        across = (1 - p.zh) * 2 + p.c
        self.across = across
        self.out = remote(part.at[across], far, sems, 2, p.far)

    def send_near(self, k):
        self.copies[k].start()

    def send_far(self):
        self.copies[0].wait()

        @pl.loop(0, 4)
        def _(k):
            rows = pl.ds(pl.multiple_of(k * 64, 64), 64)
            total = self.part[self.across, rows, :].astype(f32) + self.near[0, rows, :].astype(f32)
            self.part[self.across, rows, :] = total.astype(bf16)

        self.out.start()

    def finish(self):
        self.copies[1].wait()
        self.out.wait()

    def total(self, rows, cols):
        return (
            self.part[self.p.rank, rows, cols].astype(f32)
            + self.near[1, rows, cols].astype(f32)
            + self.far[rows, cols].astype(f32)
        )


class Exchange:
    def __init__(self, ref, me, others, sems, first, rows=None):
        at = ref.at[me] if rows is None else ref.at[me, rows]
        self.copies = [remote(at, at, sems, first + k, to) for k, to in enumerate(others)]

    def start(self):
        start_all(self.copies)

    def wait(self):
        wait_all(self.copies)


def spread(row):
    return jnp.broadcast_to(row, (128, L)).T


def row_of(total):
    return jnp.sum(total.T, axis=0, keepdims=True)


def mega_kernel(lengths, xloc, cotloc, w_z, w_x, w_bc, w_dt, w_out, norm_gain, conv_x, conv_x_bias, conv_bc, conv_bc_bias,
                dt_bias, a_log, skip_d, gate_norm,
                branch_out, gn_out, wz_grad, wx_grad, wo_grad, wbc_grad, wdt_grad, small_out,
                gain, pv, pb, hv, xg, nx, cot, wa, wz, wo, ix16, ixh, q1, q3, ibc, sraw, pre, mixed, yi, gate, gno, rgate, no, sin, bc16, rstep, S,
                dpre, dk, hs, dbc, ssx, crx, near, far, stz, got1, got2, got3,
                stb, bot3, dsend, drecv, rbc, bhalo, small, sx, sy, sz, stt, wbx,
                asem, bsem, tsem, xsem, csem, osem, gsem, esem, dsem, zsem, wsem, vsem, usem, msem, hsem):
    p = Peers()
    zh, c, me = p.zh, p.c, p.rank
    ga = WeightGather([(w_x, 0, W), (w_bc, W, 256)], wa, 640, asem, p)
    gz = WeightGather([(w_z, 0, W)], wz, 384, bsem, p)
    go = WeightGather([(w_out, 0, W)], wo, 384, tsem, p)
    ga.load()
    gz.load()
    go.load()
    dbc[0:128, 0:128] = jnp.zeros((128, 128), f32)
    dbc[0:12, 0:48] = w_dt[...].astype(f32)
    wa[p.x, p.y, ga.mine, W + 256:] = dbc[0:128, 0:128].T[0:48].astype(bf16)
    greet(p.all)
    gx = RowGather(xloc, xg, xsem, p)
    gc = RowGather(cotloc, cot, csem, p)
    ga.first()
    gx.first()
    gz.first()
    go.first()
    ends = [lengths[0, 0]]
    for k in range(1, 4):
        ends.append(ends[k - 1] + lengths[0, k])
    gain[0:1, :] = norm_gain[...].astype(f32).reshape(1, D)
    pv[0:4, :] = conv_x[...].astype(f32)
    pv[4:5, :] = conv_x_bias[...].astype(f32).reshape(1, W)
    pv[5:6, :] = gate_norm[...].astype(f32).reshape(1, W)
    skip = skip_d[...].reshape(1, 12)
    for j in range(NP):
        pv[6:7, 128 * j:128 * j + 128] = pair_cols(skip, j, iota((1, 128), 1) < 64)
    pb[0:4, :] = conv_bc[...].astype(f32)
    pb[4:5, :] = conv_bc_bias[...].astype(f32).reshape(1, 256)
    hv[...] = jnp.zeros((8, 128), f32)
    hv[0:1, 0:12] = dt_bias[...].reshape(1, 12)
    hv[1:2, 0:12] = -jnp.exp(a_log[...].reshape(1, 12))
    ixh[...] = jnp.zeros((HALO, W), f32)
    ix16[0:16, :] = jnp.zeros((16, W), bf16)
    ibc[0:HALO, :] = jnp.zeros((HALO, 256), f32)
    S[...] = jnp.zeros((N, W), f32)
    dk[...] = jnp.zeros((16, W), f32)
    hs[...] = jnp.zeros((8, 128), f32)
    small[...] = jnp.zeros((16, W), f32)
    ga.second()

    def norm_block(t):
        @pl.loop(0, 4)
        def _(k):
            rows = pl.ds(pl.multiple_of(k * 64, 64), 64)
            v = xg[t, rows, :].astype(f32)
            inv = lax.rsqrt(jnp.mean(v * v, axis=-1, keepdims=True) + 1e-05)
            nx[t, rows, :] = (v * inv * gain[0:1, :]).astype(bf16)

    gx.own.wait()
    norm_block(me)
    gx.to_near.wait()
    norm_block(zh * 2 + 1 - c)
    ga.third()
    gx.forward()
    gc.first()
    norm_block((1 - zh) * 2 + c)
    gx.finish()
    norm_block((1 - zh) * 2 + 1 - c)
    ga.forward()
    gz.second()
    ga.finish()
    gc.own.wait()
    gc.to_near.wait()
    gz.third()

    @pl.loop(0, NC)
    def _(i):
        fwd_chunk(i, ends, nx, wa, pv, pb, hv, ix16, ixh, q1, ibc, sraw, pre, mixed, yi, sin, bc16, S)

        @pl.when(i == 0)
        def _():
            gz.forward()
            go.second()

        @pl.when(i == 1)
        def _():
            gc.forward()
            go.third()

        @pl.when(i == 2)
        def _():
            go.forward()

    gz.finish()
    gc.finish()

    e_square = Exchange(ssx, me, p.group, esem, 0)
    e_cross = Exchange(crx, me, p.group, esem, 3)

    @pl.loop(0, NC)
    def _(i):
        rows = pl.ds(pl.multiple_of(i * L, L), L)
        gate[rows, :] = nn(nx[i], wz[...].reshape(D, W))
        total = jnp.zeros((L, 128), f32)
        for j in range(NP):
            cols = slice(128 * j, 128 * j + 128)
            g = gate[rows, cols]
            gated = mixed[rows, cols] * (g * sig(g))
            total = total + gated * gated
        ssx[me, :, rows] = jnp.broadcast_to(row_of(total), (8, L))

    e_square.start()
    go.finish()

    @pl.loop(0, NC)
    def _(i):
        rows = pl.ds(pl.multiple_of(i * L, L), L)
        live = iota((L, 128), 0) + i * L < ends[3]
        for j in range(2 * NP):
            cols = slice(128 * j, 128 * j + 128)
            cot[i, :, cols] = jnp.where(live, cot[i, :, cols].astype(f32), 0.0).astype(bf16)
        gno[rows, :] = nn(cot[i], wo[...].reshape(D, W))

    e_square.wait()

    def inv_of(rows):
        square = ssx[0, 0:1, rows] + ssx[1, 0:1, rows] + ssx[2, 0:1, rows] + ssx[3, 0:1, rows]
        return lax.rsqrt(square / 3072.0 + 1e-05)

    out = RowScatter(xg, near, far, osem, p)

    @pl.loop(0, NC)
    def _(i):
        t = jnp.where(i < 2, 1 - zh, zh) * 2 + jnp.where(lax.rem(i, 2) == 0, 1 - c, c)
        rows = pl.ds(pl.multiple_of(t * L, L), L)
        inv = spread(inv_of(rows))
        cross = jnp.zeros((L, 128), f32)
        for j in range(NP):
            cols = slice(128 * j, 128 * j + 128)
            g = gate[rows, cols]
            gated = mixed[rows, cols] * (g * sig(g))
            scaled = gated * inv
            gn = pv[5:6, cols]
            go = gno[rows, cols]
            no[t, :, cols] = (scaled * gn).astype(bf16)
            dk[6:7, cols] += jnp.sum(go * scaled, 0, keepdims=True)
            cross = cross + go * gn * gated
        crx[me, :, rows] = jnp.broadcast_to(row_of(cross), (8, L))
        for k in range(4):
            xg[t, :, 384 * k:384 * k + 384] = nt(no[t], wo[k].reshape(384, W)).astype(bf16)

        @pl.when(i == 0)
        def _():
            out.send_near(0)

        @pl.when(i == 2)
        def _():
            out.send_near(1)

    e_cross.start()

    def weight_part(rows_ref, grads, store):
        @pl.loop(0, 4)
        def _(b):
            left = rows_ref[:, :, pl.ds(pl.multiple_of(b * 384, 128), 384)].reshape(T, 384)
            g = grads[...].reshape(T, grads.shape[2])
            store(b, tn(left, g).astype(bf16).reshape(4, 96, grads.shape[2]))

    def store_wo(b, v):
        wo[b] = v

    weight_part(cot, no, store_wo)
    so = WeightScatter(wo, got1.at[0], got2.at[0], got3.at[0], 384, wsem, p)
    so.first()
    out.send_far()
    e_cross.wait()

    @pl.loop(0, NC)
    def _(i):
        rows = pl.ds(pl.multiple_of(i * L, L), L)
        inv_row = inv_of(rows)
        cross_row = crx[0, 0:1, rows] + crx[1, 0:1, rows] + crx[2, 0:1, rows] + crx[3, 0:1, rows]
        inv = spread(inv_row)
        back = spread(inv_row * inv_row * inv_row * cross_row / 3072.0)
        for j in range(NP):
            cols = slice(128 * j, 128 * j + 128)
            g = gate[rows, cols]
            s = sig(g)
            gs = g * s
            m = mixed[rows, cols]
            gg = inv * (gno[rows, cols] * pv[5:6, cols]) - m * gs * back
            gno[rows, cols] = gg * gs
            rgate[i, :, cols] = (gg * m * s * (1.0 + g * (1.0 - s))).astype(bf16)

    def store_z(b, v):
        stz[b] = v

    weight_part(nx, rgate, store_z)
    sz_ = WeightScatter(stz, got1.at[1], got2.at[1], got3.at[1], 384, zsem, p)
    sz_.first()

    S[...] = jnp.zeros((N, W), f32)
    dpre[...] = jnp.zeros((HALO, W), f32)
    dsend[...] = jnp.zeros((4, 512, 128), bf16)

    branch_copies = [
        pltpu.make_async_copy(gate.at[pl.ds(L * h, L), :], branch_out.at[:, pl.ds(W * h, W)], hsem.at[h]) for h in range(2)
    ]

    @pl.loop(0, NC)
    def _(i):
        bwd_chunk(NC - 1 - i, ends, pv, pb, hv, ix16, ibc, sraw, pre, mixed, yi, sin, bc16, gno,
                  S, q1, q3, dpre, no, dbc, rstep, dk, hs)
        upper = (NC - 1 - i) // 2
        part = pl.ds(pl.multiple_of(lax.rem(NC - 1 - i, 2) * L, L), L)
        half = iota((L, 128), 1) // 64
        for z in range(2):
            v = dbc[:, 128 * z:128 * z + 128]
            turned = pltpu.roll(v, 64, 1)
            for k in range(2):
                new = jnp.where(upper == k, v, turned)
                old = dsend[2 * z + k, part, :].astype(f32)
                dsend[2 * z + k, part, :] = jnp.where(half == upper, new, old).astype(bf16)

        @pl.when(i == 0)
        def _():
            so.second()
            out.finish()
            live = iota((L, 128), 0) + me * L < ends[3]
            for j in range(2 * NP):
                cols = slice(128 * j, 128 * j + 128)
                gate[L * (j // NP):L * (j // NP) + L, 128 * (j % NP):128 * (j % NP) + 128] = jnp.where(
                    live, out.total(slice(None), cols), 0.0)
            start_all(branch_copies)

        @pl.when(i == 1)
        def _():
            so.third()
            sz_.second()

        @pl.when(i == 2)
        def _():
            sz_.third()

    ranks = [zh * 2 + 1 - c, (1 - zh) * 2 + c, (1 - zh) * 2 + 1 - c]
    dcopies = [remote(dsend.at[r], drecv.at[k], dsem, k, to) for k, (r, to) in enumerate(zip(ranks, p.group))]
    start_all(dcopies)

    wo_grad[...] = so.finish()
    wz_grad[...] = sz_.finish()
    weight_part(nx, no, store_z)
    sx_ = WeightScatter(stz, got1.at[1], got2.at[1], got3.at[2], 384, vsem, p)
    sx_.first()
    wait_all(dcopies)

    bhalo[...] = jnp.zeros((HALO, 128), f32)
    tile = pl.ds(pl.multiple_of(zh * 128, 128), 128)
    half = (iota((L, 128), 1) // 64) == c

    @pl.loop(0, NC)
    def _(k):
        i = NC - 1 - k
        r0 = pl.multiple_of(i * L, L)
        part = pl.ds(pl.multiple_of(lax.rem(i, 2) * L, L), L)
        sg, masks = chunk_masks(ends, r0)
        ri = iota((L, 128), 0) + r0
        packed = dsend[me, part, :].astype(f32)
        for q in range(3):
            packed = packed + drecv[q, part, :].astype(f32)
        moved = jnp.where(i // 2 == c, packed, pltpu.roll(packed, 64, 1))
        grad = jnp.where(half, moved, 0.0)
        kernel = pb[:, tile]
        ws = taps(ibc[pl.ds(r0, L + HALO), tile], masks, HALO)
        pre_bc = kernel[4:5] + kernel[3:4] * ws[0] + kernel[2:3] * ws[1] + kernel[1:2] * ws[2] + kernel[0:1] * ws[3]
        s = sig(pre_bc)
        dp = grad * (s * (1.0 + pre_bc * (1.0 - s)))
        for t in range(4):
            cols = pl.ds(pl.multiple_of((3 - t) % 3 * 256 + zh * 128, 128), 128)
            row = 10 if t else 11
            small[row:row + 1, cols] += jnp.sum(dp * ws[t], 0, keepdims=True)
        cols = pl.ds(pl.multiple_of(256 + zh * 128, 128), 128)
        small[11:12, cols] += jnp.sum(dp, 0, keepdims=True)
        wd = jnp.concatenate([dp, bhalo[...]], axis=0)
        bhalo[...] = dp[0:HALO]
        dv = kernel[3:4] * dp
        for t in (1, 2, 3):
            same = (seg_of(ri + t, ends) == sg) & (ri + t < T)
            dv = dv + kernel[3 - t:4 - t] * jnp.where(same, wd[t:t + L], 0.0)
        rbc[0, i] = dv.astype(bf16)
        step = rstep[i].astype(f32)
        rbc[1, i] = (dv + jnp.where(half, 0.0, jnp.where(c == 0, pltpu.roll(step, 64, 1), step))).astype(bf16)

    def store_b(b, v):
        stb[b] = v

    weight_part(nx, rbc.at[1], store_b)
    low_cols = pl.ds(0, 128)
    sb_ = WeightScatter(stb, got1.at[0, :, :, :, low_cols], got2.at[0, :, :, low_cols], bot3, 128, usem, p)
    sb_.first()

    gn_sum = RowScatter(cot, near, far, gsem, p)
    small[8:10, :] = jnp.zeros((2, W), f32)

    @pl.loop(0, NC)
    def _(i):
        t = jnp.where(i < 2, 1 - zh, zh) * 2 + jnp.where(lax.rem(i, 2) == 0, 1 - c, c)
        for k in range(4):
            cols = slice(384 * k, 384 * k + 384)
            total = nt(rgate[t], wz[k].reshape(384, W))
            total = total + nt(no[t], wa[k, :, :, 0:W].reshape(384, W))
            total = total + nt(rstep[t], wa[k, :, :, W + 256:].reshape(384, 128))
            total = total + nt(rbc[0, t], wa[k, :, :, pl.ds(pl.multiple_of(W + zh * 128, 128), 128)].reshape(384, 128))
            cot[t, :, cols] = total.astype(bf16)
            weighted = jnp.sum(total * nx[t, :, cols].astype(f32), 0, keepdims=True) / gain[0:1, cols]
            small[8 + k // 2:9 + k // 2, 384 * (k % 2):384 * (k % 2) + 384] += weighted

        @pl.when(i == 0)
        def _():
            gn_sum.send_near(0)

        @pl.when(i == 1)
        def _():
            gn_sum.send_far()

        @pl.when(i == 2)
        def _():
            gn_sum.send_near(1)

    small[0:7, :] = dk[0:7, :]
    small[7:8, 0:128] = hs[0:1, :]
    small[7:8, 128:256] = hs[1:2, :]
    sx[p.x] = small[...]
    e_x = Exchange(sx, p.x, p.along_x, msem, 0)
    e_x.start()
    sx_.second()
    sb_.second()
    e_x.wait()
    sy[p.y] = sx[0] + sx[1] + sx[2] + sx[3]
    e_y = Exchange(sy, p.y, p.along_y, msem, 3)
    e_y.start()
    e_y.wait()
    sz[p.zl] = sy[0] + sy[1] + sy[2] + sy[3]
    e_z = Exchange(sz, p.zl, [p.pair], msem, 6)
    e_z.start()
    sb_.third()
    sx_.third()
    e_z.wait()
    small_out[...] = sz[0] + sz[1]
    stt[me] = small_out[8:16, :]
    e_t = Exchange(stt, me, p.group, msem, 7)
    e_t.start()
    wbx[me] = sb_.finish()
    e_b = Exchange(wbx, me, p.group, msem, 10)
    e_b.start()
    wx_grad[...] = sx_.finish()
    e_t.wait()
    small_out[8:16, :] = stt[0] + stt[1] + stt[2] + stt[3]
    e_b.wait()
    low = iota((48, 128), 1) < 64
    wbc_grad[:, 0:128] = jnp.where(low, wbx[0], wbx[1])
    wbc_grad[:, 128:256] = jnp.where(low, wbx[2], wbx[3])
    mine = wbx[me]
    wdt_grad[...] = jnp.where(c == 0, pltpu.roll(mine, 64, 1), mine)
    gn_sum.finish()
    for j in range(2 * NP):
        cols = slice(128 * j, 128 * j + 128)
        gate[L * (2 + j // NP):L * (3 + j // NP), 128 * (j % NP):128 * (j % NP) + 128] = gn_sum.total(slice(None), cols)
    gn_copies = [
        pltpu.make_async_copy(gate.at[pl.ds(L * (2 + h), L), :], gn_out.at[:, pl.ds(W * h, W)], hsem.at[2 + h])
        for h in range(2)
    ]
    start_all(gn_copies)
    wait_all(branch_copies)
    wait_all(gn_copies)


def finish_kernel(branch, gn, x_ref, cot, norm_gain, wz, wx, wo, wbc, wdt, small,
                  block_out, input_grad, gain_grad, wz_grad, wx_grad, wbc_grad, wdt_grad, conv_x, conv_x_bias, conv_bc,
                  conv_bc_bias, dt_bias, a_log, skip, gate_norm, wo_grad):
    x = x_ref[...].astype(f32)
    block_out[...] = x + branch[...]
    inv = lax.rsqrt(jnp.mean(x * x, axis=-1, keepdims=True) + 1e-05)
    g = gn[...] * norm_gain[...].astype(f32).reshape(1, D)
    inner = jnp.mean(g * x, axis=-1, keepdims=True)
    input_grad[...] = cot[...].astype(f32) + inv * g - x * (inv * inv * inv * inner)

    @pl.when(pl.program_id(0) == 0)
    def _():
        wz_grad[...] = wz[...]
        wx_grad[...] = wx[...]
        wo_grad[...] = wo[...]
        wbc_grad[...] = wbc[...]
        wdt_grad[...] = jnp.concatenate([wdt[...], jnp.zeros((80, 128), f32)], axis=0).T[0:12, 0:48]
        conv_x[...] = small[0:4, :]
        conv_x_bias[...] = small[4:5, :].reshape(W)
        he = ((iota((W, 128), 0) // 64) == iota((W, 128), 1)).astype(f32)
        sums = nn(jnp.broadcast_to(small[5:6, :], (8, W)), he, HI)
        skip[...] = sums[0:1, 0:12].reshape(12)
        gate_norm[...] = small[6:7, :].reshape(W)
        dt_bias[...] = small[7:8, 0:12].reshape(12)
        a_log[...] = small[7:8, 128:140].reshape(12)
        gain_grad[0:W] = small[8:9, :].reshape(W)
        gain_grad[W:D] = small[9:10, :].reshape(W)
        for k in range(3):
            conv_bc[k:k + 1, :] = small[10:11, 256 * k:256 * k + 256]
        conv_bc[3:4, :] = small[11:12, 0:256]
        conv_bc_bias[...] = small[11:12, 256:512].reshape(256)


vm = pl.BlockSpec(memory_space=pltpu.VMEM)
sm = pl.BlockSpec(memory_space=pltpu.SMEM)
hbm = pl.BlockSpec(memory_space=pl.ANY)
shape = jax.ShapeDtypeStruct
V = pltpu.VMEM


def sems(n):
    return pltpu.SemaphoreType.DMA((2, n))


def block(*args):
    rows4 = V((4, 256, D), bf16)
    scratch = dict(
        gain=V((8, D), f32), pv=V((16, W), f32), pb=V((8, 256), f32), hv=V((8, 128), f32), xg=rows4, nx=rows4, cot=rows4, wa=V((4, 4, 96, 1152), bf16), wz=V((4, 4, 96, W), bf16), wo=V((4, 4, 96, W), bf16),
        ix16=V((T + 16, W), bf16), ixh=V((HALO, W), f32), q1=V((L, W), f32), q3=V((L, W), f32),
        ibc=V((T + HALO, 256), f32), sraw=V((T, 128), f32), pre=V((T, W), f32), mixed=V((T, W), f32), yi=V((T, W), f32),
        gate=V((T, W), f32), gno=V((T, W), f32), rgate=V((4, L, W), bf16), no=V((4, L, W), bf16),
        sin=V((NC, N, W), bf16), bc16=V((T, 256), bf16), rstep=V((4, L, 128), bf16), S=V((N, W), f32),
        dpre=V((HALO, W), f32), dk=V((16, W), f32), hs=V((8, 128), f32), dbc=V((L, 256), f32),
        ssx=V((4, 8, T), f32), crx=V((4, 8, T), f32),
        near=V((2, L, D), bf16), far=V((L, D), bf16),
        stz=V((4, 4, 96, W), bf16), got1=V((2, 3, 4, 96, W), bf16), got2=V((2, 3, 96, W), bf16), got3=V((3, 48, W), bf16),
        stb=V((4, 4, 96, 128), bf16), bot3=V((48, 128), bf16),
        dsend=V((4, 512, 128), bf16), drecv=V((3, 512, 128), bf16), rbc=V((2, 4, L, 128), bf16), bhalo=V((HALO, 128), f32),
        small=V((16, W), f32), sx=V((4, 16, W), f32), sy=V((4, 16, W), f32), sz=V((2, 16, W), f32), stt=V((4, 8, W), f32),
        wbx=V((4, 48, 128), f32),
        asem=sems(21), bsem=sems(21), tsem=sems(21), xsem=sems(4), csem=sems(4), osem=sems(3), gsem=sems(3), esem=sems(6), dsem=sems(3),
        zsem=sems(13), wsem=sems(13), vsem=sems(13), usem=sems(13), msem=sems(13),
        hsem=pltpu.SemaphoreType.DMA((4,)),
    )
    return pl.pallas_call(
        mega_kernel,
        out_shape=[
            shape((256, D), f32), shape((256, D), f32), shape((48, W), f32), shape((48, W), f32), shape((48, W), f32),
            shape((48, 256), f32), shape((48, 128), f32), shape((16, W), f32),
        ],
        in_specs=[sm] + [hbm] * 5 + [vm, hbm] + [vm] * 9,
        out_specs=[hbm] * 2 + [vm] * 6,
        scratch_shapes=list(scratch.values()),
        compiler_params=pltpu.CompilerParams(collective_id=0, has_side_effects=True, vmem_limit_bytes=63 * 2**20),
        name="residual_block",
    )(*args)


def finish(*args):
    rows = pl.BlockSpec((64, D), lambda i: (i, 0))

    def whole(*dims):
        return pl.BlockSpec(dims, lambda i: (0,) * len(dims))

    outs = [(D,), (48, W), (48, W), (48, 256), (12, 48), (4, W), (W,), (4, 256), (256,), (12,), (12,), (12,), (W,), (48, W)]
    return pl.pallas_call(
        finish_kernel,
        grid=(4,),
        out_shape=[shape((256, D), f32)] * 2 + [shape(s, f32) for s in outs],
        in_specs=[rows] * 4 + [whole(D)] + [whole(48, W)] * 3 + [whole(48, 256), whole(48, 128), whole(16, W)],
        out_specs=[rows] * 2 + [whole(*s) for s in outs],
        name="finish",
    )(*args)


def per_device(hidden_in, norm_gain, w_z, w_x, w_bc, w_dt, conv_x, conv_x_bias, conv_bc, conv_bc_bias,
               dt_bias, a_log, skip_d, gate_norm, w_out, lengths, out_grad):
    branch, gn, wz, wx, wo, wbc, wdt, small = block(
        lengths, hidden_in, out_grad, w_z, w_x, w_bc, w_dt.T, w_out.T, norm_gain, conv_x, conv_x_bias, conv_bc, conv_bc_bias,
        dt_bias, a_log, skip_d, gate_norm)
    outs = list(finish(branch, gn, hidden_in, out_grad, norm_gain, wz, wx, wo, wbc, wdt, small))
    outs[6] = outs[6].T
    outs[15] = outs[15].T
    return tuple(outs)


def solution(mesh):
    rows, both = P(("dp", "tensor"), None), P("dp", "tensor")
    t = P("tensor")
    in_specs = (rows, P(), both, both, P("dp", None), both, P(None, "tensor"), t, P(), P(), t, t, t, t,
                P("tensor", "dp"), P("dp", None), rows)
    out_specs = (rows, rows, P(), both, both, P("dp", None), both, P(None, "tensor"), t, P(), P(), t, t, t, t,
                 P("tensor", "dp"))
    return jax.shard_map(per_device, mesh=mesh, in_specs=in_specs, out_specs=out_specs, check_vma=False)
```

```python
import jax
import jax.numpy as jnp
from jax import lax
from jax.experimental import pallas as pl
from jax.experimental.pallas import tpu as pltpu
from jax.sharding import PartitionSpec as P

f32=jnp.float32; bf16=jnp.bfloat16
T=1024; L=256; NC=4; D=1536; W=768; NP=6; N=128; HALO=8
HI=lax.Precision.HIGHEST
NEG=-1e30

def nn(a,b,prec=None): return lax.dot_general(a,b,(((1,),(0,)),((),())),precision=prec,preferred_element_type=f32)
def nt(a,b,prec=None): return lax.dot_general(a,b,(((1,),(1,)),((),())),precision=prec,preferred_element_type=f32)
def tn(a,b,prec=None): return lax.dot_general(a,b,(((0,),(0,)),((),())),precision=prec,preferred_element_type=f32)

def iota(shape,d): return lax.broadcasted_iota(jnp.int32,shape,d)
def seg_of(idx,ends):
    s=(idx>=ends[0]).astype(jnp.int32)
    for k in range(1,4): s=s+(idx>=ends[k]).astype(jnp.int32)
    return s
def sig(v): return 0.5*jnp.tanh(0.5*v)+0.5
def softplus(v): return jnp.maximum(v,0.0)+jnp.log1p(jnp.exp(-jnp.abs(v)))

def chunk_masks(ends,r0):
    ri=iota((L,128),0)+r0
    sg=seg_of(ri,ends)
    return sg,[None]+[(seg_of(ri-j,ends)==sg) for j in (1,2,3)]
def pair_cols(a,j,lo):
    return jnp.where(lo,a[:,2*j:2*j+1],a[:,2*j+1:2*j+2])
def split(v):
    high=v.astype(bf16)
    return high,(v-high.astype(f32)).astype(bf16)
def row_sums(tri,v,lane):
    a,rest=split(v)
    b=(v-a.astype(f32)-rest.astype(f32))
    packed=a.astype(f32)+pltpu.roll(rest.astype(f32),16,1)+pltpu.roll(b.astype(bf16).astype(f32),32,1)
    r=nn(tri.astype(bf16),packed.astype(bf16))
    return r+pltpu.roll(r,112,1)+pltpu.roll(r,96,1)
def taps(w,masks,halo):
    out=[w[halo:halo+L]]
    for q in (1,2,3):
        out.append(jnp.where(masks[q],w[halo-q:halo-q+L],0.0))
    return out
def conv_pre(ws,pv,kcols):
    s=pv[4:5,kcols]+pv[3:4,kcols]*ws[0]
    for q in (1,2,3): s=s+pv[3-q:4-q,kcols]*ws[q]
    return s

def head_steps(sraw,hv):
    dtp=sraw+hv[0:1,:]
    dt=softplus(dtp)
    return dtp,dt
def chunk_decay(ends,r0,dt,hv,ltri):
    dA=dt*hv[1:2,:]
    cs=row_sums(ltri,dA,None)
    return dA,cs
def seg_scalars(ends,r0):
    before=seg_of(r0-1,ends); last=seg_of(r0+L-1,ends)
    return before,last
def chunk_state_decays(cs,sg,before,last):
    e=jnp.where(sg==before,jnp.exp(cs),0.0)
    csl=cs[L-1:L,:]
    w=jnp.where(sg==last,jnp.exp(csl-cs),0.0)
    kd=jnp.exp(csl)*jnp.where(before==last,1.0,0.0)
    return e,w,kd

def fwd_chunk(c,ends,nx,wa,pv,pb,hv,ix16,ixh,tmp,ibc,sraw,pre,mixed,yi,sin,bc16,csum,S):
    r0=pl.multiple_of(c*L,L); rp=pl.multiple_of(c*L+HALO,8)
    rows=pl.ds(r0,L); rows_p=pl.ds(rp,L)
    n=nx[c]
    t=nn(n,wa[:,:,:,0:W].reshape(D,W))
    tmp[...]=t
    ix16[rows,:]=t.astype(bf16)
    t=nn(n,wa[:,:,:,W:].reshape(D,384))
    ibc[rows_p,:]=t[:,:256]
    sraw[rows,:]=t[:,256:]
    lane=iota((L,128),1); lo=lane<64
    sg,masks=chunk_masks(ends,r0)
    ti=iota((L,L),0); si=iota((L,L),1)
    mask=(seg_of(ti+r0,ends)==seg_of(si+r0,ends))&(ti>=si)
    ltri=(ti>=si).astype(f32)
    dtp,dt=head_steps(sraw[rows,:],hv)
    dA,cs=chunk_decay(ends,r0,dt,hv,ltri)
    csum[rows,:]=cs
    csT=cs.T
    before,last=seg_scalars(ends,r0)
    e,w,kd=chunk_state_decays(cs,sg,before,last)
    win=pl.ds(r0,L+HALO)
    bc=[]
    for k in range(2):
        cols=slice(128*k,128*k+128)
        p=conv_pre(taps(ibc[win,cols],masks,HALO),pb,cols)
        v=(p*sig(p)).astype(bf16)
        bc16[rows,cols]=v
        bc.append(v)
    B,C=bc
    BT=B.T
    sc=nt(C,B)
    for j in range(NP):
        cols=slice(128*j,128*j+128)
        p=conv_pre(taps(jnp.concatenate([ixh[:,cols],tmp[:,cols]],axis=0),masks,HALO),pv,cols)
        ixh[:,cols]=tmp[L-HALO:L,cols]
        pre[rows,cols]=p
        xc=p*sig(p)
        u=pair_cols(dt,j,lo)*xc
        ub=u.astype(bf16)
        y=None
        for q in range(2):
            h=2*j+q
            dec=jnp.exp(jnp.where(mask,cs[:,h:h+1]-csT[h:h+1,:],NEG))
            M=(sc*dec).astype(bf16)
            uq=jnp.where(lo if q==0 else ~lo,ub,jnp.zeros_like(ub))
            t=nn(M,uq)
            y=t if y is None else y+t
        yi[rows,cols]=y
        Sj=S[:,cols]
        Sb=Sj.astype(bf16)
        sin[c,:,cols]=Sb
        y=y+pair_cols(e,j,lo)*nn(C,Sb)
        mixed[rows,cols]=y+pv[6:7,cols]*xc
        uw=(u*pair_cols(w,j,lo)).astype(bf16)
        S[:,cols]=pair_cols(kd,j,lo[:1])*Sj+nn(BT,uw)

def bwd_chunk(c,ends,pv,pb,hv,ix16,ibc,sraw,pre,mixed,yi,sin,bc16,csum,gm,dS,
              qs,he,dpre,rx,dbc,rstep,dk,hs):
    r0=pl.multiple_of(c*L,L)
    rows=pl.ds(r0,L)
    lane=iota((L,128),1); lo=lane<64
    sg,masks=chunk_masks(ends,r0)
    ri=iota((L,128),0)+r0
    up=[None]+[((seg_of(ri+j,ends)==sg)&(ri+j<T)) for j in (1,2,3)]
    ti=iota((L,L),0); si=iota((L,L),1)
    maskT=(seg_of(ti+r0,ends)==seg_of(si+r0,ends))&(si>=ti)
    dtp,dt=head_steps(sraw[rows,:],hv)
    dA=dt*hv[1:2,:]
    cs=csum[rows,:]
    csT=cs.T
    before,last=seg_scalars(ends,r0)
    e,w,kd=chunk_state_decays(cs,sg,before,last)
    B=bc16[rows,0:128]; C=bc16[rows,128:256]
    CT=C.T
    scT=nt(B,C)
    acc=jnp.zeros((L,L),f32); dCin=jnp.zeros((L,N),f32); dBout=jnp.zeros((L,N),f32)
    rowq=[]
    for j in range(NP):
        cols=slice(128*j,128*j+128)
        g=gm[rows,cols]; gb=g.astype(bf16)
        p=pre[rows,cols]; s=sig(p); xc=p*s
        dtx=pair_cols(dt,j,lo)
        u=dtx*xc; ub=u.astype(bf16)
        sk=pv[6:7,cols]
        du=None
        for q in range(2):
            h=2*j+q
            dec=jnp.exp(jnp.where(maskT,csT[h:h+1,:]-cs[:,h:h+1],NEG))
            M=(scT*dec).astype(bf16)
            gq=jnp.where(lo if q==0 else ~lo,gb,jnp.zeros_like(gb))
            t=nn(M,gq)
            du=t if du is None else du+t
            acc=acc+nt(ub,gq)*dec
        dSj=dS[:,cols]; dSb=dSj.astype(bf16)
        Sb=sin[c,:,cols]
        wx_=pair_cols(w,j,lo); ex=pair_cols(e,j,lo)
        duo=wx_*nn(B,dSb)
        gef=g*ex
        ge=gef.astype(bf16); uw=(u*wx_).astype(bf16)
        dCin=dCin+nt(ge,Sb)
        dBout=dBout+nt(uw,dSb)
        yij=yi[rows,cols]
        y_in=mixed[rows,cols]-yij-sk*xc
        udo=u*duo
        qs[0,:,cols],qs[1,:,cols]=split((gb.astype(f32)*yij-ub.astype(f32)*du)+(g*y_in-udo))
        du=du+duo
        qs[2,:,cols],qs[3,:,cols]=split(xc*du)
        kdj=pair_cols(kd,j,lo[:1])
        rowq.append(jnp.sum(udo,0,keepdims=True)+jnp.sum(kdj*Sb.astype(f32)*dSj,0,keepdims=True))
        dS[:,cols]=kdj*dSj+nn(CT,ge)
        dxc=dtx*du+sk*g
        dp=dxc*(s*(1.0+p*(1.0-s)))
        v=ix16[rows,cols].astype(f32)
        dk[4:5,cols]+=jnp.sum(dp,0,keepdims=True)
        dk[5:6,cols]+=jnp.sum(g*xc,0,keepdims=True)
        dk[3:4,cols]+=jnp.sum(dp*v,0,keepdims=True)
        wd=jnp.concatenate([dp,dpre[:,cols]],axis=0)
        dpre[:,cols]=dp[0:HALO]
        dv=pv[3:4,cols]*dp
        for t_ in (1,2,3):
            later=jnp.where(up[t_],wd[t_:t_+L],0.0)
            dk[3-t_:4-t_,cols]+=jnp.sum(later*v,0,keepdims=True)
            dv=dv+pv[3-t_:4-t_,cols]*later
        rx[c,:,cols]=dv.astype(bf16)
    ab=acc.astype(bf16)
    dbc[:,0:128]=nn(ab,C)+dBout
    dbc[:,128:256]=nn(ab.T,B)+dCin
    own=lane<12
    r=nn(qs[0],he[0])+nn(qs[1],he[0])+nn(qs[2],he[1])+nn(qs[3],he[1])
    high,low=split(jnp.concatenate(rowq,axis=1))
    tails=jnp.concatenate([high.astype(f32),low.astype(f32),jnp.zeros((14,W),f32)],axis=0).astype(bf16)
    tails=nn(tails,he[0])
    dcs=r+jnp.where(iota((L,128),0)==L-1,tails[0:1,:]+tails[1:2,:],0.0)
    ddA=row_sums(si>=ti,jnp.where(own,dcs,0.0),None)
    ddt=pltpu.roll(r,96,1)+hv[1:2,:]*ddA
    hs[1:2,:]+=jnp.sum(ddA*dA,0,keepdims=True)
    dsr=jnp.where(own,ddt*sig(dtp),0.0)
    hs[0:1,:]+=jnp.sum(dsr,0,keepdims=True)
    rstep[c]=dsr.astype(bf16)
MESH = pl.DeviceIdType.MESH


def position():
    d = lax.axis_index("dp")
    t = lax.axis_index("tensor")
    return d // 8, (d // 2) % 4, d % 2, t // 2, t % 2


def device(x, y, zl, zh, c):
    return (lax.rem(x, 4) * 8 + lax.rem(y, 4) * 2 + zl, zh * 2 + c)


class Peers:
    def __init__(self):
        self.x, self.y, self.zl, self.zh, self.c = x, y, zl, zh, c = position()
        self.along_x = [device(x + k, y, zl, zh, c) for k in (1, 2, 3)]
        self.along_y = [device(x, y + k, zl, zh, c) for k in (1, 2, 3)]
        self.pair = device(x, y, 1 - zl, zh, c)
        self.far = device(x, y, zl, 1 - zh, c)
        self.near = device(x, y, zl, zh, 1 - c)
        self.cross = device(x, y, zl, 1 - zh, 1 - c)
        self.rank = zh * 2 + c
        self.group = [self.near, self.far, self.cross]
        self.all = self.along_x + self.along_y + [self.pair, self.far, self.near, self.cross]


def greet(devices):
    barrier = pltpu.get_barrier_semaphore()
    for other in devices:
        pl.semaphore_signal(barrier, inc=1, device_id=other, device_id_type=MESH)
    pl.semaphore_wait(barrier, len(devices))


def remote(src, dst, sems, k, to):
    return pltpu.make_async_remote_copy(
        src_ref=src, dst_ref=dst, send_sem=sems.at[0, k], recv_sem=sems.at[1, k], device_id=to, device_id_type=MESH
    )


def start_all(copies):
    for copy in copies:
        copy.start()


def wait_all(copies):
    for copy in copies:
        copy.wait()


class Ring:
    def __init__(self, at, mine, line, sems, first):
        plus, minus = line[0], line[2]
        before, after = lax.rem(mine + 3, 4), lax.rem(mine + 1, 4)
        own = [at(mine, 0), at(mine, 1)]
        self.own = [
            remote(own[0], own[0], sems, first, plus),
            remote(own[1], own[1], sems, first + 1, minus),
            remote(own[1], own[1], sems, first + 2, plus),
            remote(own[0], own[0], sems, first + 3, minus),
        ]
        self.onward = [
            remote(at(before, 0), at(before, 0), sems, first + 4, plus),
            remote(at(after, 1), at(after, 1), sems, first + 5, minus),
        ]

    def start(self):
        start_all(self.own)

    def forward(self):
        for k in range(2):
            self.own[k].wait()
            self.onward[k].start()

    def finish(self):
        wait_all(self.own[2:])
        wait_all(self.onward)


class WeightGather:
    def __init__(self, pieces, full, split, sems, p):
        x, y = p.x, p.y
        cols = full.shape[3]
        a, b = pl.ds(0, split), pl.ds(split, cols - split)
        mine = pl.ds(pl.multiple_of(p.zl * 48, 16), 48)
        self.mine = mine
        self.z = remote(full.at[x, y, mine, :], full.at[x, y, mine, :], sems, 0, p.pair)
        self.own = [
            pltpu.make_async_copy(piece, full.at[x, y, mine, pl.ds(at, width)], sems.at[0, 19 + k])
            for k, (piece, at, width) in enumerate(pieces)
        ]
        self.mid = []
        for k in range(3):
            ya, xb = full.at[x, y, :, a], full.at[x, y, :, b]
            self.mid.append(remote(ya, ya, sems, 1 + k, p.along_y[k]))
            self.mid.append(remote(xb, xb, sems, 4 + k, p.along_x[k]))
        self.last = [
            Ring(lambda o, h: full.at[o, pl.ds(2 * h, 2), :, a], x, p.along_x, sems, 7),
            Ring(lambda o, h: full.at[pl.ds(2 * h, 2), o, :, b], y, p.along_y, sems, 13),
        ]

    def load(self):
        start_all(self.own)

    def first(self):
        wait_all(self.own)
        self.z.start()

    def second(self):
        self.z.wait()
        start_all(self.mid)

    def third(self):
        wait_all(self.mid)
        start_all(self.last)

    def forward(self):
        for ring in self.last:
            ring.forward()

    def finish(self):
        for ring in self.last:
            ring.finish()


class WeightScatter:
    def __init__(self, part, got1, got2, got3, split, sems, p):
        x, y = p.x, p.y
        cols = got3.shape[1]
        self.part, self.got1, self.got2, self.got3, self.p = part, got1, got2, got3, p
        self.a, self.b = a, b = pl.ds(0, split), pl.ds(split, cols - split)
        mine = pl.ds(pl.multiple_of(p.zl * 48, 16), 48)
        other = pl.ds(pl.multiple_of((1 - p.zl) * 48, 16), 48)
        self.mine = mine
        self.one = []
        self.two = []
        for k in range(3):
            xk, yk = lax.rem(x + k + 1, 4), lax.rem(y + k + 1, 4)
            self.one.append(remote(part.at[xk, :, :, a], got1.at[k, :, :, a], sems, k, p.along_x[k]))
            if b.size:
                self.one.append(remote(part.at[:, yk, :, b], got1.at[k, :, :, b], sems, 3 + k, p.along_y[k]))
            self.two.append(remote(part.at[x, yk, :, a], got2.at[k, :, a], sems, 6 + k, p.along_y[k]))
            if b.size:
                self.two.append(remote(part.at[xk, y, :, b], got2.at[k, :, b], sems, 9 + k, p.along_x[k]))
        self.three = remote(part.at[x, y, other, :], got3, sems, 12, p.pair)

    def first(self):
        start_all(self.one)

    def second(self):
        wait_all(self.one)
        x, y, part, got = self.p.x, self.p.y, self.part, self.got1

        @pl.loop(0, 4)
        def _(i):
            for cut, at in ((self.a, (x, i)), (self.b, (i, y))):
                if cut.size:
                    total = part[at[0], at[1], :, cut].astype(f32)
                    for k in range(3):
                        total = total + got[k, i, :, cut].astype(f32)
                    part[at[0], at[1], :, cut] = total.astype(bf16)

        start_all(self.two)

    def third(self):
        wait_all(self.two)
        total = self.part[self.p.x, self.p.y].astype(f32)
        for k in range(3):
            total = total + self.got2[k].astype(f32)
        self.part[self.p.x, self.p.y] = total.astype(bf16)
        self.three.start()

    def finish(self):
        self.three.wait()
        return self.part[self.p.x, self.p.y, self.mine, :].astype(f32) + self.got3[...].astype(f32)


class RowGather:
    def __init__(self, own, full, sems, p):
        me, across = p.rank, (1 - p.zh) * 2 + p.c
        self.to_far = remote(own, full.at[me], sems, 0, p.far)
        self.to_near = remote(own, full.at[me], sems, 1, p.near)
        self.onward = remote(full.at[across], full.at[across], sems, 2, p.near)
        self.own = pltpu.make_async_copy(own, full.at[me], sems.at[0, 3])

    def first(self):
        self.to_far.start()
        self.to_near.start()
        self.own.start()

    def forward(self):
        self.to_far.wait()
        self.onward.start()

    def finish(self):
        self.onward.wait()


class RowScatter:
    def __init__(self, part, near, far, sems, p):
        self.part, self.near, self.far, self.p = part, near, far, p
        self.copies = [
            remote(part.at[z * 2 + 1 - p.c], near.at[k], sems, k, p.near)
            for k, z in ((0, 1 - p.zh), (1, p.zh))
        ]
        across = (1 - p.zh) * 2 + p.c
        self.across = across
        self.out = remote(part.at[across], far, sems, 2, p.far)

    def send_near(self, k):
        self.copies[k].start()

    def send_far(self):
        self.copies[0].wait_recv()

        @pl.loop(0, 4)
        def _(k):
            rows = pl.ds(pl.multiple_of(k * 64, 64), 64)
            total = self.part[self.across, rows, :].astype(f32) + self.near[0, rows, :].astype(f32)
            self.part[self.across, rows, :] = total.astype(bf16)

        self.out.start()

    def finish(self):
        self.copies[0].wait_send()
        self.copies[1].wait()
        self.out.wait()

    def total(self, rows, cols):
        return (
            self.part[self.p.rank, rows, cols].astype(f32)
            + self.near[1, rows, cols].astype(f32)
            + self.far[rows, cols].astype(f32)
        )


class Exchange:
    def __init__(self, ref, me, others, sems, first, rows=None):
        at = ref.at[me] if rows is None else ref.at[me, rows]
        self.copies = [remote(at, at, sems, first + k, to) for k, to in enumerate(others)]

    def start(self):
        start_all(self.copies)

    def wait(self):
        wait_all(self.copies)


def spread(row):
    return jnp.broadcast_to(row, (128, L)).T


def row_of(total):
    return jnp.sum(total.T, axis=0, keepdims=True)


def mega_kernel(lengths, xloc, cotloc, w_z, w_x, w_bc, w_dt, w_out, norm_gain, conv_x, conv_x_bias, conv_bc, conv_bc_bias,
                dt_bias, a_log, skip_d, gate_norm,
                branch_out, gn_out, wz_grad, wx_grad, wo_grad, wbc_grad, wdt_grad, small_out,
                gain, pv, pb, hv, xg, nx, cot, wa, wz, wo, ix16, ixh, qs, he, csum, ibc, sraw, pre, mixed, yi, gate, gno, rgate, no, sin, bc16, rstep, S,
                dpre, dk, hs, dbc, ssx, crx, near, far, stz, got1, got2, got3,
                stb, bot3, dsend, drecv, rmix, bhalo, small, ax, ay, az, bt, bz, bx, by, wbx,
                asem, bsem, tsem, xsem, csem, osem, gsem, esem, dsem, zsem, wsem, vsem, usem, msem, hsem):
    p = Peers()
    zh, c, me = p.zh, p.c, p.rank
    ga = WeightGather([(w_x, 0, W), (w_bc, W, 256)], wa, 640, asem, p)
    gz = WeightGather([(w_z, 0, W)], wz, 384, bsem, p)
    go = WeightGather([(w_out, 0, W)], wo, 384, tsem, p)
    ga.load()
    gz.load()
    go.load()
    dbc[0:128, 0:128] = jnp.zeros((128, 128), f32)
    dbc[0:12, 0:48] = w_dt[...].astype(f32)
    wa[p.x, p.y, ga.mine, W + 256:] = dbc[0:128, 0:128].T[0:48].astype(bf16)
    greet(p.all)
    gx = RowGather(xloc, xg, xsem, p)
    gc = RowGather(cotloc, cot, csem, p)
    ga.first()
    gx.first()
    gz.first()
    go.first()
    ends = [lengths[0, 0]]
    for k in range(1, 4):
        ends.append(ends[k - 1] + lengths[0, k])
    gain[0:1, :] = norm_gain[...].astype(f32).reshape(1, D)
    pv[0:4, :] = conv_x[...].astype(f32)
    pv[4:5, :] = conv_x_bias[...].astype(f32).reshape(1, W)
    pv[5:6, :] = gate_norm[...].astype(f32).reshape(1, W)
    skip = skip_d[...].reshape(1, 12)
    for j in range(NP):
        pv[6:7, 128 * j:128 * j + 128] = pair_cols(skip, j, iota((1, 128), 1) < 64)
    pb[0:4, :] = conv_bc[...].astype(f32)
    pb[4:5, :] = conv_bc_bias[...].astype(f32).reshape(1, 256)
    hv[...] = jnp.zeros((8, 128), f32)
    hv[0:1, 0:12] = dt_bias[...].reshape(1, 12)
    hv[1:2, 0:12] = -jnp.exp(a_log[...].reshape(1, 12))
    ixh[...] = jnp.zeros((HALO, W), f32)
    lane = iota((W, 128), 1)
    head = iota((W, 128), 0) // 64
    he[0] = jnp.where(lane == head, 1.0, 0.0).astype(bf16)
    he[1] = jnp.where(lane == head + 32, 1.0, 0.0).astype(bf16)
    ibc[0:HALO, :] = jnp.zeros((HALO, 256), f32)
    S[...] = jnp.zeros((N, W), f32)
    dk[...] = jnp.zeros((16, W), f32)
    hs[...] = jnp.zeros((8, 128), f32)
    small[...] = jnp.zeros((16, W), f32)
    ga.second()

    def norm_block(t):
        @pl.loop(0, 4)
        def _(k):
            rows = pl.ds(pl.multiple_of(k * 64, 64), 64)
            v = xg[t, rows, :].astype(f32)
            inv = lax.rsqrt(jnp.mean(v * v, axis=-1, keepdims=True) + 1e-05)
            nx[t, rows, :] = (v * inv * gain[0:1, :]).astype(bf16)

    gx.own.wait()
    norm_block(me)
    gx.to_near.wait()
    norm_block(zh * 2 + 1 - c)
    ga.third()
    gx.forward()
    gc.first()
    norm_block((1 - zh) * 2 + c)
    gx.finish()
    norm_block((1 - zh) * 2 + 1 - c)
    ga.forward()
    gz.second()
    ga.finish()
    gc.own.wait()
    gc.to_near.wait()
    gz.third()

    @pl.loop(0, NC)
    def _(i):
        fwd_chunk(i, ends, nx, wa, pv, pb, hv, ix16, ixh, gate.at[pl.ds(0, L), :], ibc, sraw, pre, mixed, yi, sin, bc16, csum, S)

        @pl.when(i == 0)
        def _():
            gz.forward()
            go.second()

        @pl.when(i == 1)
        def _():
            gc.forward()
            go.third()

        @pl.when(i == 2)
        def _():
            go.forward()

    gz.finish()
    gc.finish()

    e_square = Exchange(ssx, me, p.group, esem, 0)
    e_cross = Exchange(crx, me, p.group, esem, 3)

    @pl.loop(0, NC)
    def _(i):
        rows = pl.ds(pl.multiple_of(i * L, L), L)
        gate[rows, :] = nn(nx[i], wz[...].reshape(D, W))
        total = jnp.zeros((L, 128), f32)
        for j in range(NP):
            cols = slice(128 * j, 128 * j + 128)
            g = gate[rows, cols]
            gated = mixed[rows, cols] * (g * sig(g))
            total = total + gated * gated
        ssx[me, :, rows] = jnp.broadcast_to(row_of(total), (8, L))

    e_square.start()
    go.finish()

    @pl.loop(0, NC)
    def _(i):
        rows = pl.ds(pl.multiple_of(i * L, L), L)
        live = iota((L, 128), 0) + i * L < ends[3]
        for j in range(2 * NP):
            cols = slice(128 * j, 128 * j + 128)
            cot[i, :, cols] = jnp.where(live, cot[i, :, cols].astype(f32), 0.0).astype(bf16)
        gno[rows, :] = nn(cot[i], wo[...].reshape(D, W))

    e_square.wait()

    def inv_of(rows):
        square = ssx[0, 0:1, rows] + ssx[1, 0:1, rows] + ssx[2, 0:1, rows] + ssx[3, 0:1, rows]
        return lax.rsqrt(square / 3072.0 + 1e-05)

    out = RowScatter(xg, near, far, osem, p)

    @pl.loop(0, NC)
    def _(i):
        t = jnp.where(i < 2, 1 - zh, zh) * 2 + jnp.where(lax.rem(i, 2) == 0, 1 - c, c)
        rows = pl.ds(pl.multiple_of(t * L, L), L)
        inv = spread(inv_of(rows))
        cross = jnp.zeros((L, 128), f32)
        for j in range(NP):
            cols = slice(128 * j, 128 * j + 128)
            g = gate[rows, cols]
            gated = mixed[rows, cols] * (g * sig(g))
            scaled = gated * inv
            gn = pv[5:6, cols]
            go = gno[rows, cols]
            no[t, :, cols] = (scaled * gn).astype(bf16)
            dk[6:7, cols] += jnp.sum(go * scaled, 0, keepdims=True)
            cross = cross + go * gn * gated
        crx[me, :, rows] = jnp.broadcast_to(row_of(cross), (8, L))
        for k in range(2):
            xg[t, :, W * k:W * k + W] = nt(no[t], wo[2 * k:2 * k + 2].reshape(W, W)).astype(bf16)

        @pl.when(i == 0)
        def _():
            out.send_near(0)

        @pl.when(i == 2)
        def _():
            out.send_near(1)

    e_cross.start()
    out.send_far()

    def weight_part(rows_ref, grads, store):
        @pl.loop(0, 4)
        def _(b):
            left = rows_ref[:, :, pl.ds(pl.multiple_of(b * 384, 128), 384)].reshape(T, 384)
            g = grads[...].reshape(T, grads.shape[2])
            store(b, tn(left, g).astype(bf16).reshape(4, 96, grads.shape[2]))

    def store_wo(b, v):
        wo[b] = v

    weight_part(cot, no, store_wo)
    so = WeightScatter(wo, got1.at[0], got2.at[0], got3.at[0], 384, wsem, p)
    so.first()
    e_cross.wait()

    @pl.loop(0, NC)
    def _(i):
        rows = pl.ds(pl.multiple_of(i * L, L), L)
        inv_row = inv_of(rows)
        cross_row = crx[0, 0:1, rows] + crx[1, 0:1, rows] + crx[2, 0:1, rows] + crx[3, 0:1, rows]
        inv = spread(inv_row)
        back = spread(inv_row * inv_row * inv_row * cross_row / 3072.0)
        for j in range(NP):
            cols = slice(128 * j, 128 * j + 128)
            g = gate[rows, cols]
            s = sig(g)
            gs = g * s
            m = mixed[rows, cols]
            gg = inv * (gno[rows, cols] * pv[5:6, cols]) - m * gs * back
            gno[rows, cols] = gg * gs
            rgate[i, :, cols] = (gg * m * s * (1.0 + g * (1.0 - s))).astype(bf16)

    def store_z(b, v):
        stz[b] = v

    weight_part(nx, rgate, store_z)
    sz_ = WeightScatter(stz, got1.at[1], got2.at[1], got3.at[1], 384, zsem, p)
    sz_.first()

    S[...] = jnp.zeros((N, W), f32)
    dpre[...] = jnp.zeros((HALO, W), f32)

    branch_copies = [
        pltpu.make_async_copy(gate.at[pl.ds(L * h, L), :], branch_out.at[:, pl.ds(W * h, W)], hsem.at[h]) for h in range(2)
    ]

    ranks = [zh * 2 + 1 - c, (1 - zh) * 2 + c, (1 - zh) * 2 + 1 - c]
    tile = pl.ds(pl.multiple_of(zh * 128, 128), 128)
    half = (iota((L, 128), 1) // 64) == c
    bhalo[...] = jnp.zeros((HALO, 128), f32)
    for k in range(4):
        bc_tile = wa[k, :, :, pl.ds(pl.multiple_of(W + zh * 128, 128), 128)].reshape(384, 128).astype(f32)
        dt_tile = wa[k, :, :, W + 256:].reshape(384, 128).astype(f32)
        dt_tile = jnp.where(c == 0, pltpu.roll(dt_tile, 64, 1), dt_tile)
        mix = jnp.where((iota((384, 128), 1) // 64) == c, bc_tile, dt_tile)
        stb[k] = mix.astype(bf16).reshape(4, 96, 128)
    gn_sum = RowScatter(cot, near, far, gsem, p)
    across = (1 - zh) * 2 + c

    def bc_copies(q):
        return [remote(dsend.at[q, r], drecv.at[q, k], dsem, 3 * q + k, to) for k, (r, to) in enumerate(zip(ranks, p.group))]

    def pack(q):
        low = iota((128, 128), 1) < 64
        for z in range(2):
            cols = slice(128 * z, 128 * z + 128)
            top, bottom = dbc[0:128, cols], dbc[128:256, cols]
            dsend[q, 2 * z] = jnp.where(low, top, pltpu.roll(bottom, 64, 1)).astype(bf16)
            dsend[q, 2 * z + 1] = jnp.where(low, pltpu.roll(top, 64, 1), bottom).astype(bf16)

    def conv_back(q):
        r0 = pl.multiple_of(q * L, L)
        sg, masks = chunk_masks(ends, r0)
        ri = iota((L, 128), 0) + r0
        packed = dsend[q, me].astype(f32)
        for k in range(3):
            packed = packed + drecv[q, k].astype(f32)
        turned = pltpu.roll(packed, 64, 1)
        both = jnp.concatenate([jnp.where(c == 0, packed, turned), jnp.where(c == 0, turned, packed)], axis=0)
        grad = jnp.where(half, both, 0.0)
        kernel = pb[:, tile]
        ws = taps(ibc[pl.ds(r0, L + HALO), tile], masks, HALO)
        pre_bc = kernel[4:5] + kernel[3:4] * ws[0] + kernel[2:3] * ws[1] + kernel[1:2] * ws[2] + kernel[0:1] * ws[3]
        s = sig(pre_bc)
        dp = grad * (s * (1.0 + pre_bc * (1.0 - s)))
        cols = pl.ds(pl.multiple_of(256 + zh * 128, 128), 128)
        small[11:12, cols] += jnp.sum(dp, 0, keepdims=True)
        wd = jnp.concatenate([dp, bhalo[...]], axis=0)
        bhalo[...] = dp[0:HALO]
        dv = jnp.zeros((L, 128), f32)
        for t in range(4):
            later = dp
            if t:
                later = jnp.where((seg_of(ri + t, ends) == sg) & (ri + t < T), wd[t:t + L], 0.0)
            dv = dv + kernel[3 - t:4 - t] * later
            cols = pl.ds(pl.multiple_of((3 - t) % 3 * 256 + zh * 128, 128), 128)
            row = 10 if t else 11
            small[row:row + 1, cols] += jnp.sum(later * ws[0], 0, keepdims=True)
        step = rstep[q].astype(f32)
        rmix[q] = (dv + jnp.where(half, 0.0, jnp.where(c == 0, pltpu.roll(step, 64, 1), step))).astype(bf16)

    def normed_grad(q):
        for k in range(2):
            cols = slice(W * k, W * k + W)
            total = nt(rgate[q], wz[2 * k:2 * k + 2].reshape(W, W))
            total = total + nt(no[q], wa[2 * k:2 * k + 2, :, :, 0:W].reshape(W, W))
            total = total + nt(rmix[q], stb[2 * k:2 * k + 2].reshape(W, 128))
            cot[q, :, cols] = total.astype(bf16)
            weighted = jnp.sum(total * nx[q, :, cols].astype(f32), 0, keepdims=True) / gain[0:1, cols]
            small[8 + k:9 + k, :] += weighted

        @pl.when(q == (1 - zh) * 2 + 1 - c)
        def _():
            gn_sum.send_near(0)

        @pl.when(q == zh * 2 + 1 - c)
        def _():
            gn_sum.send_near(1)

    branch_copies = [
        pltpu.make_async_copy(gate.at[pl.ds(L * h, L), :], branch_out.at[:, pl.ds(W * h, W)], hsem.at[h]) for h in range(2)
    ]
    a_x = Exchange(ax, p.x, p.along_x, msem, 0)
    a_y = Exchange(ay, p.y, p.along_y, msem, 3)
    a_z = Exchange(az, p.zl, [p.pair], msem, 6)
    b_t = Exchange(bt, me, p.group, msem, 7)
    b_z = Exchange(bz, p.zl, [p.pair], msem, 10)
    b_x = Exchange(bx, p.x, p.along_x, msem, 11)
    b_y = Exchange(by, p.y, p.along_y, msem, 14)
    sx_ = WeightScatter(wo, got1.at[0], got2.at[0], got3.at[2], 384, vsem, p)

    @pl.loop(0, NC + 1)
    def _(i):
        @pl.when(i < NC)
        def _():
            q = NC - 1 - i
            bwd_chunk(q, ends, pv, pb, hv, ix16, ibc, sraw, pre, mixed, yi, sin, bc16, csum, gno,
                      S, qs, he, dpre, no, dbc, rstep, dk, hs)
            pack(q)

            @pl.when(i == 0)
            def _():
                out.finish()
                live = iota((L, 128), 0) + me * L < ends[3]
                for j in range(2 * NP):
                    cols = slice(128 * j, 128 * j + 128)
                    gate[L * (j // NP):L * (j // NP) + L, 128 * (j % NP):128 * (j % NP) + 128] = jnp.where(
                        live, out.total(slice(None), cols), 0.0)
                start_all(branch_copies)

            start_all(bc_copies(q))

            @pl.when(i == 1)
            def _():
                so.second()

            @pl.when(i == 2)
            def _():
                so.third()
                sz_.second()

            @pl.when(i == 3)
            def _():
                sz_.third()

        @pl.when(i == NC)
        def _():
            small[0:7, :] = dk[0:7, :]
            small[7:8, 0:128] = hs[0:1, :]
            small[7:8, 128:256] = hs[1:2, :]
            ax[p.x] = small[0:8, :]
            a_x.start()
            wo_grad[...] = so.finish()
            weight_part(nx, no, store_wo)
            a_x.wait()
            ay[p.y] = ax[0] + ax[1] + ax[2] + ax[3]
            a_y.start()
            sx_.first()

        @pl.when((i > 1) & (NC + 1 - i == across))
        def _():
            gn_sum.send_far()

        @pl.when(i > 0)
        def _():
            wait_all(bc_copies(NC - i))
            conv_back(NC - i)
            normed_grad(NC - i)

    bt[me] = small[8:16, :]
    b_t.start()

    def store_b(b, v):
        stb[b] = v

    weight_part(nx, rmix, store_b)
    low_cols = pl.ds(0, 128)
    sb_ = WeightScatter(stb, got1.at[1, :, :, :, low_cols], got2.at[1, :, :, low_cols], bot3, 128, usem, p)
    sb_.first()

    @pl.when(across == 0)
    def _():
        gn_sum.send_far()

    a_y.wait()
    az[p.zl] = ay[0] + ay[1] + ay[2] + ay[3]
    a_z.start()
    b_t.wait()
    bz[p.zl] = bt[0] + bt[1] + bt[2] + bt[3]
    b_z.start()
    wz_grad[...] = sz_.finish()
    a_z.wait()
    small_out[0:8, :] = az[0] + az[1]
    b_z.wait()
    bx[p.x] = bz[0] + bz[1]
    b_x.start()
    sb_.second()
    sx_.second()
    b_x.wait()
    by[p.y] = bx[0] + bx[1] + bx[2] + bx[3]
    b_y.start()
    sb_.third()
    sx_.third()
    b_y.wait()
    small_out[8:16, :] = by[0] + by[1] + by[2] + by[3]
    wbx[me] = sb_.finish()
    e_b = Exchange(wbx, me, p.group, msem, 17)
    e_b.start()
    wx_grad[...] = sx_.finish()
    gn_sum.finish()
    for j in range(2 * NP):
        cols = slice(128 * j, 128 * j + 128)
        gate[L * (2 + j // NP):L * (3 + j // NP), 128 * (j % NP):128 * (j % NP) + 128] = gn_sum.total(slice(None), cols)
    gn_copies = [
        pltpu.make_async_copy(gate.at[pl.ds(L * (2 + h), L), :], gn_out.at[:, pl.ds(W * h, W)], hsem.at[2 + h])
        for h in range(2)
    ]
    start_all(gn_copies)
    e_b.wait()
    low = iota((48, 128), 1) < 64
    wbc_grad[:, 0:128] = jnp.where(low, wbx[0], wbx[1])
    wbc_grad[:, 128:256] = jnp.where(low, wbx[2], wbx[3])
    mine = wbx[me]
    wdt_grad[...] = jnp.where(c == 0, pltpu.roll(mine, 64, 1), mine)
    wait_all(branch_copies)
    wait_all(gn_copies)


def finish_kernel(branch, gn, x_ref, cot, norm_gain, wz, wx, wo, wbc, wdt, small,
                  block_out, input_grad, gain_grad, wz_grad, wx_grad, wbc_grad, wdt_grad, conv_x, conv_x_bias, conv_bc,
                  conv_bc_bias, dt_bias, a_log, skip, gate_norm, wo_grad):
    x = x_ref[...].astype(f32)
    block_out[...] = x + branch[...]
    inv = lax.rsqrt(jnp.mean(x * x, axis=-1, keepdims=True) + 1e-05)
    g = gn[...] * norm_gain[...].astype(f32).reshape(1, D)
    inner = jnp.mean(g * x, axis=-1, keepdims=True)
    input_grad[...] = cot[...].astype(f32) + inv * g - x * (inv * inv * inv * inner)

    @pl.when(pl.program_id(0) == 0)
    def _():
        wz_grad[...] = wz[...]
        wx_grad[...] = wx[...]
        wo_grad[...] = wo[...]
        wbc_grad[...] = wbc[...]
        wdt_grad[...] = jnp.concatenate([wdt[...], jnp.zeros((80, 128), f32)], axis=0).T[0:12, 0:48]
        conv_x[...] = small[0:4, :]
        conv_x_bias[...] = small[4:5, :].reshape(W)
        he = ((iota((W, 128), 0) // 64) == iota((W, 128), 1)).astype(f32)
        sums = nn(jnp.broadcast_to(small[5:6, :], (8, W)), he, HI)
        skip[...] = sums[0:1, 0:12].reshape(12)
        gate_norm[...] = small[6:7, :].reshape(W)
        dt_bias[...] = small[7:8, 0:12].reshape(12)
        a_log[...] = small[7:8, 128:140].reshape(12)
        gain_grad[0:W] = small[8:9, :].reshape(W)
        gain_grad[W:D] = small[9:10, :].reshape(W)
        for k in range(3):
            conv_bc[k:k + 1, :] = small[10:11, 256 * k:256 * k + 256]
        conv_bc[3:4, :] = small[11:12, 0:256]
        conv_bc_bias[...] = small[11:12, 256:512].reshape(256)


vm = pl.BlockSpec(memory_space=pltpu.VMEM)
sm = pl.BlockSpec(memory_space=pltpu.SMEM)
hbm = pl.BlockSpec(memory_space=pl.ANY)
shape = jax.ShapeDtypeStruct
V = pltpu.VMEM


def sems(n):
    return pltpu.SemaphoreType.DMA((2, n))


def block(*args):
    rows4 = V((4, 256, D), bf16)
    scratch = dict(
        gain=V((8, D), f32), pv=V((16, W), f32), pb=V((8, 256), f32), hv=V((8, 128), f32), xg=rows4, nx=rows4, cot=rows4, wa=V((4, 4, 96, 1152), bf16), wz=V((4, 4, 96, W), bf16), wo=V((4, 4, 96, W), bf16),
        ix16=V((T, W), bf16), ixh=V((HALO, W), f32), qs=V((4, L, W), bf16), he=V((2, W, 128), bf16), csum=V((T, 128), f32),
        ibc=V((T + HALO, 256), f32), sraw=V((T, 128), f32), pre=V((T, W), f32), mixed=V((T, W), f32), yi=V((T, W), f32),
        gate=V((T, W), f32), gno=V((T, W), f32), rgate=V((4, L, W), bf16), no=V((4, L, W), bf16),
        sin=V((NC, N, W), bf16), bc16=V((T, 256), bf16), rstep=V((4, L, 128), bf16), S=V((N, W), f32),
        dpre=V((HALO, W), f32), dk=V((16, W), f32), hs=V((8, 128), f32), dbc=V((L, 256), f32),
        ssx=V((4, 8, T), f32), crx=V((4, 8, T), f32),
        near=V((2, L, D), bf16), far=V((L, D), bf16),
        stz=V((4, 4, 96, W), bf16), got1=V((2, 3, 4, 96, W), bf16), got2=V((2, 3, 96, W), bf16), got3=V((3, 48, W), bf16),
        stb=V((4, 4, 96, 128), bf16), bot3=V((48, 128), bf16),
        dsend=V((4, 4, 128, 128), bf16), drecv=V((4, 3, 128, 128), bf16), rmix=V((4, L, 128), bf16), bhalo=V((HALO, 128), f32),
        small=V((16, W), f32), ax=V((4, 8, W), f32), ay=V((4, 8, W), f32), az=V((2, 8, W), f32), bt=V((4, 8, W), f32), bz=V((2, 8, W), f32),
        bx=V((4, 8, W), f32), by=V((4, 8, W), f32),
        wbx=V((4, 48, 128), f32),
        asem=sems(21), bsem=sems(21), tsem=sems(21), xsem=sems(4), csem=sems(4), osem=sems(3), gsem=sems(3), esem=sems(6), dsem=sems(12),
        zsem=sems(13), wsem=sems(13), vsem=sems(13), usem=sems(13), msem=sems(20),
        hsem=pltpu.SemaphoreType.DMA((4,)),
    )
    return pl.pallas_call(
        mega_kernel,
        out_shape=[
            shape((256, D), f32), shape((256, D), f32), shape((48, W), f32), shape((48, W), f32), shape((48, W), f32),
            shape((48, 256), f32), shape((48, 128), f32), shape((16, W), f32),
        ],
        in_specs=[sm] + [hbm] * 5 + [vm, hbm] + [vm] * 9,
        out_specs=[hbm] * 2 + [vm] * 6,
        scratch_shapes=list(scratch.values()),
        compiler_params=pltpu.CompilerParams(collective_id=0, has_side_effects=True, vmem_limit_bytes=63 * 2**20),
        name="residual_block",
    )(*args)


def finish(*args):
    rows = pl.BlockSpec((64, D), lambda i: (i, 0))

    def whole(*dims):
        return pl.BlockSpec(dims, lambda i: (0,) * len(dims))

    outs = [(D,), (48, W), (48, W), (48, 256), (12, 48), (4, W), (W,), (4, 256), (256,), (12,), (12,), (12,), (W,), (48, W)]
    return pl.pallas_call(
        finish_kernel,
        grid=(4,),
        out_shape=[shape((256, D), f32)] * 2 + [shape(s, f32) for s in outs],
        in_specs=[rows] * 4 + [whole(D)] + [whole(48, W)] * 3 + [whole(48, 256), whole(48, 128), whole(16, W)],
        out_specs=[rows] * 2 + [whole(*s) for s in outs],
        name="finish",
    )(*args)


def per_device(hidden_in, norm_gain, w_z, w_x, w_bc, w_dt, conv_x, conv_x_bias, conv_bc, conv_bc_bias,
               dt_bias, a_log, skip_d, gate_norm, w_out, lengths, out_grad):
    branch, gn, wz, wx, wo, wbc, wdt, small = block(
        lengths, hidden_in, out_grad, w_z, w_x, w_bc, w_dt.T, w_out.T, norm_gain, conv_x, conv_x_bias, conv_bc, conv_bc_bias,
        dt_bias, a_log, skip_d, gate_norm)
    outs = list(finish(branch, gn, hidden_in, out_grad, norm_gain, wz, wx, wo, wbc, wdt, small))
    outs[6] = outs[6].T
    outs[15] = outs[15].T
    return tuple(outs)


def solution(mesh):
    rows, both = P(("dp", "tensor"), None), P("dp", "tensor")
    t = P("tensor")
    in_specs = (rows, P(), both, both, P("dp", None), both, P(None, "tensor"), t, P(), P(), t, t, t, t,
                P("tensor", "dp"), P("dp", None), rows)
    out_specs = (rows, rows, P(), both, both, P("dp", None), both, P(None, "tensor"), t, P(), P(), t, t, t, t,
                 P("tensor", "dp"))
    return jax.shard_map(per_device, mesh=mesh, in_specs=in_specs, out_specs=out_specs, check_vma=False)
```

```python
import jax
import jax.numpy as jnp
from jax import lax
from jax.experimental import pallas as pl
from jax.experimental.pallas import tpu as pltpu
from jax.sharding import PartitionSpec as P

f32=jnp.float32; bf16=jnp.bfloat16
T=1024; L=256; NC=4; D=1536; W=768; NP=6; N=128; HALO=8
HI=lax.Precision.HIGHEST
NEG=-1e30

def nn(a,b,prec=None): return lax.dot_general(a,b,(((1,),(0,)),((),())),precision=prec,preferred_element_type=f32)
def nt(a,b,prec=None): return lax.dot_general(a,b,(((1,),(1,)),((),())),precision=prec,preferred_element_type=f32)
def tn(a,b,prec=None): return lax.dot_general(a,b,(((0,),(0,)),((),())),precision=prec,preferred_element_type=f32)

def iota(shape,d): return lax.broadcasted_iota(jnp.int32,shape,d)
def seg_of(idx,ends):
    s=(idx>=ends[0]).astype(jnp.int32)
    for k in range(1,4): s=s+(idx>=ends[k]).astype(jnp.int32)
    return s
def sig(v): return 0.5*jnp.tanh(0.5*v)+0.5
def softplus(v): return jnp.maximum(v,0.0)+jnp.log1p(jnp.exp(-jnp.abs(v)))

def chunk_masks(ends,r0):
    ri=iota((L,128),0)+r0
    sg=seg_of(ri,ends)
    return sg,[None]+[(seg_of(ri-j,ends)==sg) for j in (1,2,3)]
def pair_cols(a,j,lo):
    return jnp.where(lo,a[:,2*j:2*j+1],a[:,2*j+1:2*j+2])
def split(v):
    high=v.astype(bf16)
    return high,(v-high.astype(f32)).astype(bf16)
def row_sums(tri,v,lane):
    a,rest=split(v)
    b=(v-a.astype(f32)-rest.astype(f32))
    packed=a.astype(f32)+pltpu.roll(rest.astype(f32),16,1)+pltpu.roll(b.astype(bf16).astype(f32),32,1)
    r=nn(tri.astype(bf16),packed.astype(bf16))
    return r+pltpu.roll(r,112,1)+pltpu.roll(r,96,1)
def taps(w,masks,halo):
    out=[w[halo:halo+L]]
    for q in (1,2,3):
        out.append(jnp.where(masks[q],w[halo-q:halo-q+L],0.0))
    return out
def conv_pre(ws,pv,kcols):
    s=pv[4:5,kcols]+pv[3:4,kcols]*ws[0]
    for q in (1,2,3): s=s+pv[3-q:4-q,kcols]*ws[q]
    return s

def head_steps(sraw,hv):
    dtp=sraw+hv[0:1,:]
    dt=softplus(dtp)
    return dtp,dt
def chunk_decay(ends,r0,dt,hv,ltri):
    dA=dt*hv[1:2,:]
    cs=row_sums(ltri,dA,None)
    return dA,cs
def seg_scalars(ends,r0):
    before=seg_of(r0-1,ends); last=seg_of(r0+L-1,ends)
    return before,last
def chunk_state_decays(cs,sg,before,last):
    e=jnp.where(sg==before,jnp.exp(cs),0.0)
    csl=cs[L-1:L,:]
    w=jnp.where(sg==last,jnp.exp(csl-cs),0.0)
    kd=jnp.exp(csl)*jnp.where(before==last,1.0,0.0)
    return e,w,kd

def fwd_chunk(c,ends,nx,wa,pv,pb,hv,ix16,ixh,tmp,ibc,sraw,pre,mixed,yi,sin,bc16,csum,S):
    r0=pl.multiple_of(c*L,L); rp=pl.multiple_of(c*L+HALO,8)
    rows=pl.ds(r0,L); rows_p=pl.ds(rp,L)
    n=nx[c]
    t=nn(n,wa[:,:,:,0:W].reshape(D,W))
    tmp[...]=t
    ix16[rows,:]=t.astype(bf16)
    t=nn(n,wa[:,:,:,W:].reshape(D,384))
    ibc[rows_p,:]=t[:,:256]
    sraw[rows,:]=t[:,256:]
    lane=iota((L,128),1); lo=lane<64
    sg,masks=chunk_masks(ends,r0)
    ti=iota((L,L),0); si=iota((L,L),1)
    mask=(seg_of(ti+r0,ends)==seg_of(si+r0,ends))&(ti>=si)
    ltri=(ti>=si).astype(f32)
    dtp,dt=head_steps(sraw[rows,:],hv)
    dA,cs=chunk_decay(ends,r0,dt,hv,ltri)
    csum[rows,:]=cs
    csT=cs.T
    before,last=seg_scalars(ends,r0)
    e,w,kd=chunk_state_decays(cs,sg,before,last)
    win=pl.ds(r0,L+HALO)
    bc=[]
    for k in range(2):
        cols=slice(128*k,128*k+128)
        p=conv_pre(taps(ibc[win,cols],masks,HALO),pb,cols)
        v=(p*sig(p)).astype(bf16)
        bc16[rows,cols]=v
        bc.append(v)
    B,C=bc
    BT=B.T
    sc=nt(C,B)
    for j in range(NP):
        cols=slice(128*j,128*j+128)
        p=conv_pre(taps(jnp.concatenate([ixh[:,cols],tmp[:,cols]],axis=0),masks,HALO),pv,cols)
        ixh[:,cols]=tmp[L-HALO:L,cols]
        pre[rows,cols]=p
        xc=p*sig(p)
        u=pair_cols(dt,j,lo)*xc
        ub=u.astype(bf16)
        y=None
        for q in range(2):
            h=2*j+q
            dec=jnp.exp(jnp.where(mask,cs[:,h:h+1]-csT[h:h+1,:],NEG))
            M=(sc*dec).astype(bf16)
            uq=jnp.where(lo if q==0 else ~lo,ub,jnp.zeros_like(ub))
            t=nn(M,uq)
            y=t if y is None else y+t
        yi[rows,cols]=y
        Sj=S[:,cols]
        Sb=Sj.astype(bf16)
        sin[c,:,cols]=Sb
        y=y+pair_cols(e,j,lo)*nn(C,Sb)
        mixed[rows,cols]=y+pv[6:7,cols]*xc
        uw=(u*pair_cols(w,j,lo)).astype(bf16)
        S[:,cols]=pair_cols(kd,j,lo[:1])*Sj+nn(BT,uw)

def bwd_chunk(c,ends,pv,pb,hv,ix16,ibc,sraw,pre,mixed,yi,sin,bc16,csum,gm,dS,
              qs,he,dpre,rx,dbc,rstep,dk,hs):
    r0=pl.multiple_of(c*L,L)
    rows=pl.ds(r0,L)
    lane=iota((L,128),1); lo=lane<64
    sg,masks=chunk_masks(ends,r0)
    ri=iota((L,128),0)+r0
    up=[None]+[((seg_of(ri+j,ends)==sg)&(ri+j<T)) for j in (1,2,3)]
    ti=iota((L,L),0); si=iota((L,L),1)
    maskT=(seg_of(ti+r0,ends)==seg_of(si+r0,ends))&(si>=ti)
    dtp,dt=head_steps(sraw[rows,:],hv)
    dA=dt*hv[1:2,:]
    cs=csum[rows,:]
    csT=cs.T
    before,last=seg_scalars(ends,r0)
    e,w,kd=chunk_state_decays(cs,sg,before,last)
    B=bc16[rows,0:128]; C=bc16[rows,128:256]
    CT=C.T
    scT=nt(B,C)
    acc=jnp.zeros((L,L),f32); dCin=jnp.zeros((L,N),f32); dBout=jnp.zeros((L,N),f32)
    rowq=[]
    for j in range(NP):
        cols=slice(128*j,128*j+128)
        g=gm[rows,cols]; gb=g.astype(bf16)
        p=pre[rows,cols]; s=sig(p); xc=p*s
        dtx=pair_cols(dt,j,lo)
        u=dtx*xc; ub=u.astype(bf16)
        sk=pv[6:7,cols]
        du=None
        for q in range(2):
            h=2*j+q
            dec=jnp.exp(jnp.where(maskT,csT[h:h+1,:]-cs[:,h:h+1],NEG))
            M=(scT*dec).astype(bf16)
            gq=jnp.where(lo if q==0 else ~lo,gb,jnp.zeros_like(gb))
            t=nn(M,gq)
            du=t if du is None else du+t
            acc=acc+nt(ub,gq)*dec
        dSj=dS[:,cols]; dSb=dSj.astype(bf16)
        Sb=sin[c,:,cols]
        wx_=pair_cols(w,j,lo); ex=pair_cols(e,j,lo)
        duo=wx_*nn(B,dSb)
        gef=g*ex
        ge=gef.astype(bf16); uw=(u*wx_).astype(bf16)
        dCin=dCin+nt(ge,Sb)
        dBout=dBout+nt(uw,dSb)
        yij=yi[rows,cols]
        y_in=mixed[rows,cols]-yij-sk*xc
        udo=u*duo
        qs[0,:,cols],qs[1,:,cols]=split((gb.astype(f32)*yij-ub.astype(f32)*du)+(g*y_in-udo))
        du=du+duo
        qs[2,:,cols],qs[3,:,cols]=split(xc*du)
        kdj=pair_cols(kd,j,lo[:1])
        rowq.append(jnp.sum(udo,0,keepdims=True)+jnp.sum(kdj*Sb.astype(f32)*dSj,0,keepdims=True))
        dS[:,cols]=kdj*dSj+nn(CT,ge)
        dxc=dtx*du+sk*g
        dp=dxc*(s*(1.0+p*(1.0-s)))
        v=ix16[rows,cols].astype(f32)
        dk[4:5,cols]+=jnp.sum(dp,0,keepdims=True)
        dk[5:6,cols]+=jnp.sum(g*xc,0,keepdims=True)
        dk[3:4,cols]+=jnp.sum(dp*v,0,keepdims=True)
        wd=jnp.concatenate([dp,dpre[:,cols]],axis=0)
        dpre[:,cols]=dp[0:HALO]
        dv=pv[3:4,cols]*dp
        for t_ in (1,2,3):
            later=jnp.where(up[t_],wd[t_:t_+L],0.0)
            dk[3-t_:4-t_,cols]+=jnp.sum(later*v,0,keepdims=True)
            dv=dv+pv[3-t_:4-t_,cols]*later
        rx[c,:,cols]=dv.astype(bf16)
    ab=acc.astype(bf16)
    dbc[:,0:128]=nn(ab,C)+dBout
    dbc[:,128:256]=nn(ab.T,B)+dCin
    own=lane<12
    r=nn(qs[0],he[0])+nn(qs[1],he[0])+nn(qs[2],he[1])+nn(qs[3],he[1])
    high,low=split(jnp.concatenate(rowq,axis=1))
    tails=jnp.concatenate([high.astype(f32),low.astype(f32),jnp.zeros((14,W),f32)],axis=0).astype(bf16)
    tails=nn(tails,he[0])
    dcs=r+jnp.where(iota((L,128),0)==L-1,tails[0:1,:]+tails[1:2,:],0.0)
    ddA=row_sums(si>=ti,jnp.where(own,dcs,0.0),None)
    ddt=pltpu.roll(r,96,1)+hv[1:2,:]*ddA
    hs[1:2,:]+=jnp.sum(ddA*dA,0,keepdims=True)
    dsr=jnp.where(own,ddt*sig(dtp),0.0)
    hs[0:1,:]+=jnp.sum(dsr,0,keepdims=True)
    rstep[c]=dsr.astype(bf16)
MESH = pl.DeviceIdType.MESH


def position():
    d = lax.axis_index("dp")
    t = lax.axis_index("tensor")
    return d // 8, (d // 2) % 4, d % 2, t // 2, t % 2


def device(x, y, zl, zh, c):
    return (lax.rem(x, 4) * 8 + lax.rem(y, 4) * 2 + zl, zh * 2 + c)


class Peers:
    def __init__(self):
        self.x, self.y, self.zl, self.zh, self.c = x, y, zl, zh, c = position()
        self.along_x = [device(x + k, y, zl, zh, c) for k in (1, 2, 3)]
        self.along_y = [device(x, y + k, zl, zh, c) for k in (1, 2, 3)]
        self.pair = device(x, y, 1 - zl, zh, c)
        self.far = device(x, y, zl, 1 - zh, c)
        self.near = device(x, y, zl, zh, 1 - c)
        self.cross = device(x, y, zl, 1 - zh, 1 - c)
        self.rank = zh * 2 + c
        self.group = [self.near, self.far, self.cross]
        self.all = self.along_x + self.along_y + [self.pair, self.far, self.near, self.cross]


def greet(devices):
    barrier = pltpu.get_barrier_semaphore()
    for other in devices:
        pl.semaphore_signal(barrier, inc=1, device_id=other, device_id_type=MESH)
    pl.semaphore_wait(barrier, len(devices))


def remote(src, dst, sems, k, to):
    return pltpu.make_async_remote_copy(
        src_ref=src, dst_ref=dst, send_sem=sems.at[0, k], recv_sem=sems.at[1, k], device_id=to, device_id_type=MESH
    )


def start_all(copies):
    for copy in copies:
        copy.start()


def wait_all(copies):
    for copy in copies:
        copy.wait()


class Ring:
    def __init__(self, at, mine, line, sems, first):
        plus, minus = line[0], line[2]
        before, after = lax.rem(mine + 3, 4), lax.rem(mine + 1, 4)
        own = [at(mine, 0), at(mine, 1)]
        self.own = [
            remote(own[0], own[0], sems, first, plus),
            remote(own[1], own[1], sems, first + 1, minus),
            remote(own[1], own[1], sems, first + 2, plus),
            remote(own[0], own[0], sems, first + 3, minus),
        ]
        self.onward = [
            remote(at(before, 0), at(before, 0), sems, first + 4, plus),
            remote(at(after, 1), at(after, 1), sems, first + 5, minus),
        ]

    def start(self):
        start_all(self.own)

    def forward(self):
        for k in range(2):
            self.own[k].wait()
            self.onward[k].start()

    def finish(self):
        wait_all(self.own[2:])
        wait_all(self.onward)


class WeightGather:
    def __init__(self, pieces, full, split, sems, p):
        x, y = p.x, p.y
        cols = full.shape[3]
        a, b = pl.ds(0, split), pl.ds(split, cols - split)
        mine = pl.ds(pl.multiple_of(p.zl * 48, 16), 48)
        self.mine = mine
        self.z = remote(full.at[x, y, mine, :], full.at[x, y, mine, :], sems, 0, p.pair)
        self.own = [
            pltpu.make_async_copy(piece, full.at[x, y, mine, pl.ds(at, width)], sems.at[0, 19 + k])
            for k, (piece, at, width) in enumerate(pieces)
        ]
        self.mid = []
        for k in range(3):
            ya, xb = full.at[x, y, :, a], full.at[x, y, :, b]
            self.mid.append(remote(ya, ya, sems, 1 + k, p.along_y[k]))
            self.mid.append(remote(xb, xb, sems, 4 + k, p.along_x[k]))
        self.last = [
            Ring(lambda o, h: full.at[o, pl.ds(2 * h, 2), :, a], x, p.along_x, sems, 7),
            Ring(lambda o, h: full.at[pl.ds(2 * h, 2), o, :, b], y, p.along_y, sems, 13),
        ]

    def load(self):
        start_all(self.own)

    def first(self):
        wait_all(self.own)
        self.z.start()

    def second(self):
        self.z.wait()
        start_all(self.mid)

    def third(self):
        wait_all(self.mid)
        start_all(self.last)

    def forward(self):
        for ring in self.last:
            ring.forward()

    def finish(self):
        for ring in self.last:
            ring.finish()


class WeightScatter:
    def __init__(self, part, got1, got2, got3, split, sems, p):
        x, y = p.x, p.y
        cols = got3.shape[1]
        self.part, self.got1, self.got2, self.got3, self.p = part, got1, got2, got3, p
        self.a, self.b = a, b = pl.ds(0, split), pl.ds(split, cols - split)
        mine = pl.ds(pl.multiple_of(p.zl * 48, 16), 48)
        other = pl.ds(pl.multiple_of((1 - p.zl) * 48, 16), 48)
        self.mine = mine
        self.one = []
        self.two = []
        for k in range(3):
            xk, yk = lax.rem(x + k + 1, 4), lax.rem(y + k + 1, 4)
            self.one.append(remote(part.at[xk, :, :, a], got1.at[k, :, :, a], sems, k, p.along_x[k]))
            if b.size:
                self.one.append(remote(part.at[:, yk, :, b], got1.at[k, :, :, b], sems, 3 + k, p.along_y[k]))
            self.two.append(remote(part.at[x, yk, :, a], got2.at[k, :, a], sems, 6 + k, p.along_y[k]))
            if b.size:
                self.two.append(remote(part.at[xk, y, :, b], got2.at[k, :, b], sems, 9 + k, p.along_x[k]))
        self.three = remote(part.at[x, y, other, :], got3, sems, 12, p.pair)

    def first(self):
        start_all(self.one)

    def second(self):
        wait_all(self.one)
        x, y, part, got = self.p.x, self.p.y, self.part, self.got1

        @pl.loop(0, 4)
        def _(i):
            for cut, at in ((self.a, (x, i)), (self.b, (i, y))):
                if cut.size:
                    total = part[at[0], at[1], :, cut].astype(f32)
                    for k in range(3):
                        total = total + got[k, i, :, cut].astype(f32)
                    part[at[0], at[1], :, cut] = total.astype(bf16)

        start_all(self.two)

    def third(self):
        wait_all(self.two)
        total = self.part[self.p.x, self.p.y].astype(f32)
        for k in range(3):
            total = total + self.got2[k].astype(f32)
        self.part[self.p.x, self.p.y] = total.astype(bf16)
        self.three.start()

    def finish(self):
        self.three.wait()
        return self.part[self.p.x, self.p.y, self.mine, :].astype(f32) + self.got3[...].astype(f32)


class RowGather:
    def __init__(self, own, full, sems, p):
        me, across = p.rank, (1 - p.zh) * 2 + p.c
        self.to_far = remote(own, full.at[me], sems, 0, p.far)
        self.to_near = remote(own, full.at[me], sems, 1, p.near)
        self.onward = remote(full.at[across], full.at[across], sems, 2, p.near)
        self.own = pltpu.make_async_copy(own, full.at[me], sems.at[0, 3])

    def first(self):
        self.to_far.start()
        self.to_near.start()
        self.own.start()

    def forward(self):
        self.to_far.wait()
        self.onward.start()

    def finish(self):
        self.onward.wait()


class RowScatter:
    def __init__(self, part, near, far, sems, p):
        self.part, self.near, self.far, self.p = part, near, far, p
        self.copies = [
            remote(part.at[z * 2 + 1 - p.c], near.at[k], sems, k, p.near)
            for k, z in ((0, 1 - p.zh), (1, p.zh))
        ]
        across = (1 - p.zh) * 2 + p.c
        self.across = across
        self.out = remote(part.at[across], far, sems, 2, p.far)

    def send_near(self, k):
        self.copies[k].start()

    def send_far(self):
        self.copies[0].wait_recv()

        @pl.loop(0, 4)
        def _(k):
            rows = pl.ds(pl.multiple_of(k * 64, 64), 64)
            total = self.part[self.across, rows, :].astype(f32) + self.near[0, rows, :].astype(f32)
            self.part[self.across, rows, :] = total.astype(bf16)

        self.out.start()

    def finish(self):
        self.copies[0].wait_send()
        self.copies[1].wait()
        self.out.wait()

    def total(self, rows, cols):
        return (
            self.part[self.p.rank, rows, cols].astype(f32)
            + self.near[1, rows, cols].astype(f32)
            + self.far[rows, cols].astype(f32)
        )


class Exchange:
    def __init__(self, ref, me, others, sems, first, rows=None):
        at = ref.at[me] if rows is None else ref.at[me, rows]
        self.copies = [remote(at, at, sems, first + k, to) for k, to in enumerate(others)]

    def start(self):
        start_all(self.copies)

    def wait(self):
        wait_all(self.copies)


def spread(row):
    return jnp.broadcast_to(row, (128, L)).T


def row_of(total):
    return jnp.sum(total.T, axis=0, keepdims=True)


def mega_kernel(lengths, xloc, cotloc, w_z, w_x, w_bc, w_dt, w_out, norm_gain, conv_x, conv_x_bias, conv_bc, conv_bc_bias,
                dt_bias, a_log, skip_d, gate_norm,
                branch_out, gn_out, wz_grad, wx_grad, wo_grad, wbc_grad, wdt_grad, small_out,
                gain, pv, pb, hv, xg, nx, cot, wa, wz, wo, ix16, ixh, qs, he, csum, ibc, sraw, pre, mixed, yi, gate, gno, rgate, no, sin, bc16, rstep, S,
                dpre, dk, hs, dbc, ssx, crx, near, far, stz, got1, got2, got3,
                stb, bot3, dsend, drecv, rmix, bhalo, small, ax, ay, az, bt, bz, bx, by, wbx,
                asem, bsem, tsem, xsem, csem, osem, gsem, esem, dsem, zsem, wsem, vsem, usem, msem, hsem):
    p = Peers()
    zh, c, me = p.zh, p.c, p.rank
    ga = WeightGather([(w_x, 0, W), (w_bc, W, 256)], wa, 640, asem, p)
    gz = WeightGather([(w_z, 0, W)], wz, 384, bsem, p)
    go = WeightGather([(w_out, 0, W)], wo, 384, tsem, p)
    ga.load()
    gz.load()
    go.load()
    dbc[0:128, 0:128] = jnp.zeros((128, 128), f32)
    dbc[0:12, 0:48] = w_dt[...].astype(f32)
    wa[p.x, p.y, ga.mine, W + 256:] = dbc[0:128, 0:128].T[0:48].astype(bf16)
    greet(p.all)
    gx = RowGather(xloc, xg, xsem, p)
    gc = RowGather(cotloc, cot, csem, p)
    ga.first()
    gx.first()
    gz.first()
    go.first()
    ends = [lengths[0, 0]]
    for k in range(1, 4):
        ends.append(ends[k - 1] + lengths[0, k])
    gain[0:1, :] = norm_gain[...].astype(f32).reshape(1, D)
    pv[0:4, :] = conv_x[...].astype(f32)
    pv[4:5, :] = conv_x_bias[...].astype(f32).reshape(1, W)
    pv[5:6, :] = gate_norm[...].astype(f32).reshape(1, W)
    skip = skip_d[...].reshape(1, 12)
    for j in range(NP):
        pv[6:7, 128 * j:128 * j + 128] = pair_cols(skip, j, iota((1, 128), 1) < 64)
    pb[0:4, :] = conv_bc[...].astype(f32)
    pb[4:5, :] = conv_bc_bias[...].astype(f32).reshape(1, 256)
    hv[...] = jnp.zeros((8, 128), f32)
    hv[0:1, 0:12] = dt_bias[...].reshape(1, 12)
    hv[1:2, 0:12] = -jnp.exp(a_log[...].reshape(1, 12))
    ixh[...] = jnp.zeros((HALO, W), f32)
    lane = iota((W, 128), 1)
    head = iota((W, 128), 0) // 64
    he[0] = jnp.where(lane == head, 1.0, 0.0).astype(bf16)
    he[1] = jnp.where(lane == head + 32, 1.0, 0.0).astype(bf16)
    ibc[0:HALO, :] = jnp.zeros((HALO, 256), f32)
    S[...] = jnp.zeros((N, W), f32)
    dk[...] = jnp.zeros((16, W), f32)
    hs[...] = jnp.zeros((8, 128), f32)
    small[...] = jnp.zeros((16, W), f32)
    ga.second()

    def norm_block(t):
        @pl.loop(0, 4)
        def _(k):
            rows = pl.ds(pl.multiple_of(k * 64, 64), 64)
            v = xg[t, rows, :].astype(f32)
            inv = lax.rsqrt(jnp.mean(v * v, axis=-1, keepdims=True) + 1e-05)
            nx[t, rows, :] = (v * inv * gain[0:1, :]).astype(bf16)

    gx.own.wait()
    norm_block(me)
    gx.to_near.wait()
    norm_block(zh * 2 + 1 - c)
    ga.third()
    gx.forward()
    gc.first()
    norm_block((1 - zh) * 2 + c)
    gx.finish()
    norm_block((1 - zh) * 2 + 1 - c)
    ga.forward()
    gz.second()
    ga.finish()
    gc.own.wait()
    gc.to_near.wait()
    gz.third()

    @pl.loop(0, NC)
    def _(i):
        fwd_chunk(i, ends, nx, wa, pv, pb, hv, ix16, ixh, gate.at[pl.ds(0, L), :], ibc, sraw, pre, mixed, yi, sin, bc16, csum, S)

        @pl.when(i == 0)
        def _():
            gz.forward()
            go.second()

        @pl.when(i == 1)
        def _():
            gc.forward()
            go.third()

        @pl.when(i == 2)
        def _():
            go.forward()

    gz.finish()
    gc.finish()

    e_square = Exchange(ssx, me, p.group, esem, 0)
    e_cross = Exchange(crx, me, p.group, esem, 3)

    @pl.loop(0, NC)
    def _(i):
        rows = pl.ds(pl.multiple_of(i * L, L), L)
        gate[rows, :] = nn(nx[i], wz[...].reshape(D, W))
        total = jnp.zeros((L, 128), f32)
        for j in range(NP):
            cols = slice(128 * j, 128 * j + 128)
            g = gate[rows, cols]
            gated = mixed[rows, cols] * (g * sig(g))
            total = total + gated * gated
        ssx[me, :, rows] = jnp.broadcast_to(row_of(total), (8, L))

    e_square.start()
    go.finish()

    @pl.loop(0, NC)
    def _(i):
        rows = pl.ds(pl.multiple_of(i * L, L), L)
        live = iota((L, 128), 0) + i * L < ends[3]
        for j in range(2 * NP):
            cols = slice(128 * j, 128 * j + 128)
            cot[i, :, cols] = jnp.where(live, cot[i, :, cols].astype(f32), 0.0).astype(bf16)
        gno[rows, :] = nn(cot[i], wo[...].reshape(D, W))

    e_square.wait()

    def inv_of(rows):
        square = ssx[0, 0:1, rows] + ssx[1, 0:1, rows] + ssx[2, 0:1, rows] + ssx[3, 0:1, rows]
        return lax.rsqrt(square / 3072.0 + 1e-05)

    out = RowScatter(xg, near, far, osem, p)

    @pl.loop(0, NC)
    def _(i):
        t = jnp.where(i < 2, 1 - zh, zh) * 2 + jnp.where(lax.rem(i, 2) == 0, 1 - c, c)
        rows = pl.ds(pl.multiple_of(t * L, L), L)
        inv = spread(inv_of(rows))
        cross = jnp.zeros((L, 128), f32)
        for j in range(NP):
            cols = slice(128 * j, 128 * j + 128)
            g = gate[rows, cols]
            gated = mixed[rows, cols] * (g * sig(g))
            scaled = gated * inv
            gn = pv[5:6, cols]
            go = gno[rows, cols]
            no[t, :, cols] = (scaled * gn).astype(bf16)
            dk[6:7, cols] += jnp.sum(go * scaled, 0, keepdims=True)
            cross = cross + go * gn * gated
        crx[me, :, rows] = jnp.broadcast_to(row_of(cross), (8, L))
        for k in range(2):
            xg[t, :, W * k:W * k + W] = nt(no[t], wo[2 * k:2 * k + 2].reshape(W, W)).astype(bf16)

        @pl.when(i == 0)
        def _():
            out.send_near(0)

        @pl.when(i == 2)
        def _():
            out.send_near(1)

    e_cross.start()
    out.send_far()

    def weight_part(rows_ref, grads, store):
        @pl.loop(0, 4)
        def _(b):
            left = rows_ref[:, :, pl.ds(pl.multiple_of(b * 384, 128), 384)].reshape(T, 384)
            g = grads[...].reshape(T, grads.shape[2])
            store(b, tn(left, g).astype(bf16).reshape(4, 96, grads.shape[2]))

    def store_wo(b, v):
        wo[b] = v

    weight_part(cot, no, store_wo)
    so = WeightScatter(wo, got1.at[0], got2.at[0], got3.at[0], 384, wsem, p)
    so.first()
    e_cross.wait()

    @pl.loop(0, NC)
    def _(i):
        rows = pl.ds(pl.multiple_of(i * L, L), L)
        inv_row = inv_of(rows)
        cross_row = crx[0, 0:1, rows] + crx[1, 0:1, rows] + crx[2, 0:1, rows] + crx[3, 0:1, rows]
        inv = spread(inv_row)
        back = spread(inv_row * inv_row * inv_row * cross_row / 3072.0)
        for j in range(NP):
            cols = slice(128 * j, 128 * j + 128)
            g = gate[rows, cols]
            s = sig(g)
            gs = g * s
            m = mixed[rows, cols]
            gg = inv * (gno[rows, cols] * pv[5:6, cols]) - m * gs * back
            gno[rows, cols] = gg * gs
            rgate[i, :, cols] = (gg * m * s * (1.0 + g * (1.0 - s))).astype(bf16)

    def store_z(b, v):
        stz[b] = v

    weight_part(nx, rgate, store_z)
    sz_ = WeightScatter(stz, got1.at[1], got2.at[1], got3.at[1], 384, zsem, p)
    sz_.first()

    S[...] = jnp.zeros((N, W), f32)
    dpre[...] = jnp.zeros((HALO, W), f32)

    branch_copies = [
        pltpu.make_async_copy(gate.at[pl.ds(L * h, L), :], branch_out.at[:, pl.ds(W * h, W)], hsem.at[h]) for h in range(2)
    ]

    ranks = [zh * 2 + 1 - c, (1 - zh) * 2 + c, (1 - zh) * 2 + 1 - c]
    tile = pl.ds(pl.multiple_of(zh * 128, 128), 128)
    half = (iota((L, 128), 1) // 64) == c
    bhalo[...] = jnp.zeros((HALO, 128), f32)
    for k in range(4):
        bc_tile = wa[k, :, :, pl.ds(pl.multiple_of(W + zh * 128, 128), 128)].reshape(384, 128).astype(f32)
        dt_tile = wa[k, :, :, W + 256:].reshape(384, 128).astype(f32)
        dt_tile = jnp.where(c == 0, pltpu.roll(dt_tile, 64, 1), dt_tile)
        mix = jnp.where((iota((384, 128), 1) // 64) == c, bc_tile, dt_tile)
        stb[k] = mix.astype(bf16).reshape(4, 96, 128)
    gn_sum = RowScatter(cot, near, far, gsem, p)
    across = (1 - zh) * 2 + c

    def bc_copies(q):
        return [remote(dsend.at[q, r], drecv.at[q, k], dsem, 3 * q + k, to) for k, (r, to) in enumerate(zip(ranks, p.group))]

    def pack(q):
        low = iota((128, 128), 1) < 64
        for z in range(2):
            cols = slice(128 * z, 128 * z + 128)
            top, bottom = dbc[0:128, cols], dbc[128:256, cols]
            dsend[q, 2 * z] = jnp.where(low, top, pltpu.roll(bottom, 64, 1)).astype(bf16)
            dsend[q, 2 * z + 1] = jnp.where(low, pltpu.roll(top, 64, 1), bottom).astype(bf16)

    def conv_back(q):
        r0 = pl.multiple_of(q * L, L)
        sg, masks = chunk_masks(ends, r0)
        ri = iota((L, 128), 0) + r0
        packed = dsend[q, me].astype(f32)
        for k in range(3):
            packed = packed + drecv[q, k].astype(f32)
        turned = pltpu.roll(packed, 64, 1)
        both = jnp.concatenate([jnp.where(c == 0, packed, turned), jnp.where(c == 0, turned, packed)], axis=0)
        grad = jnp.where(half, both, 0.0)
        kernel = pb[:, tile]
        ws = taps(ibc[pl.ds(r0, L + HALO), tile], masks, HALO)
        pre_bc = kernel[4:5] + kernel[3:4] * ws[0] + kernel[2:3] * ws[1] + kernel[1:2] * ws[2] + kernel[0:1] * ws[3]
        s = sig(pre_bc)
        dp = grad * (s * (1.0 + pre_bc * (1.0 - s)))
        cols = pl.ds(pl.multiple_of(256 + zh * 128, 128), 128)
        small[11:12, cols] += jnp.sum(dp, 0, keepdims=True)
        wd = jnp.concatenate([dp, bhalo[...]], axis=0)
        bhalo[...] = dp[0:HALO]
        dv = jnp.zeros((L, 128), f32)
        for t in range(4):
            later = dp
            if t:
                later = jnp.where((seg_of(ri + t, ends) == sg) & (ri + t < T), wd[t:t + L], 0.0)
            dv = dv + kernel[3 - t:4 - t] * later
            cols = pl.ds(pl.multiple_of((3 - t) % 3 * 256 + zh * 128, 128), 128)
            row = 10 if t else 11
            small[row:row + 1, cols] += jnp.sum(later * ws[0], 0, keepdims=True)
        step = rstep[q].astype(f32)
        rmix[q] = (dv + jnp.where(half, 0.0, jnp.where(c == 0, pltpu.roll(step, 64, 1), step))).astype(bf16)

    def normed_grad(q):
        for k in range(2):
            cols = slice(W * k, W * k + W)
            total = nt(rgate[q], wz[2 * k:2 * k + 2].reshape(W, W))
            total = total + nt(no[q], wa[2 * k:2 * k + 2, :, :, 0:W].reshape(W, W))
            total = total + nt(rmix[q], stb[2 * k:2 * k + 2].reshape(W, 128))
            cot[q, :, cols] = total.astype(bf16)
            weighted = jnp.sum(total * nx[q, :, cols].astype(f32), 0, keepdims=True) / gain[0:1, cols]
            small[8 + k:9 + k, :] += weighted

        @pl.when(q == (1 - zh) * 2 + 1 - c)
        def _():
            gn_sum.send_near(0)

        @pl.when(q == zh * 2 + 1 - c)
        def _():
            gn_sum.send_near(1)

    branch_copies = [
        pltpu.make_async_copy(gate.at[pl.ds(L * h, L), :], branch_out.at[:, pl.ds(W * h, W)], hsem.at[h]) for h in range(2)
    ]
    a_x = Exchange(ax, p.x, p.along_x, msem, 0)
    a_y = Exchange(ay, p.y, p.along_y, msem, 3)
    a_z = Exchange(az, p.zl, [p.pair], msem, 6)
    b_t = Exchange(bt, me, p.group, msem, 7)
    b_z = Exchange(bz, p.zl, [p.pair], msem, 10)
    b_x = Exchange(bx, p.x, p.along_x, msem, 11)
    b_y = Exchange(by, p.y, p.along_y, msem, 14)
    sx_ = WeightScatter(wo, got1.at[0], got2.at[0], got3.at[2], 384, vsem, p)

    @pl.loop(0, NC + 1)
    def _(i):
        @pl.when(i < NC)
        def _():
            q = NC - 1 - i
            bwd_chunk(q, ends, pv, pb, hv, ix16, ibc, sraw, pre, mixed, yi, sin, bc16, csum, gno,
                      S, qs, he, dpre, no, dbc, rstep, dk, hs)
            pack(q)

            @pl.when(i == 0)
            def _():
                out.finish()
                live = iota((L, 128), 0) + me * L < ends[3]
                for j in range(2 * NP):
                    cols = slice(128 * j, 128 * j + 128)
                    gate[L * (j // NP):L * (j // NP) + L, 128 * (j % NP):128 * (j % NP) + 128] = jnp.where(
                        live, out.total(slice(None), cols), 0.0)
                start_all(branch_copies)

            start_all(bc_copies(q))

            @pl.when(i == 1)
            def _():
                so.second()

            @pl.when(i == 2)
            def _():
                so.third()
                sz_.second()

            @pl.when(i == 3)
            def _():
                sz_.third()

        @pl.when(i == NC)
        def _():
            small[0:7, :] = dk[0:7, :]
            small[7:8, 0:128] = hs[0:1, :]
            small[7:8, 128:256] = hs[1:2, :]
            ax[p.x] = small[0:8, :]
            a_x.start()
            wo_grad[...] = so.finish()
            weight_part(nx, no, store_wo)
            a_x.wait()
            ay[p.y] = ax[0] + ax[1] + ax[2] + ax[3]
            a_y.start()
            sx_.first()

        @pl.when((i > 1) & (NC + 1 - i == across))
        def _():
            gn_sum.send_far()

        @pl.when(i > 0)
        def _():
            wait_all(bc_copies(NC - i))
            conv_back(NC - i)
            normed_grad(NC - i)

    bt[me] = small[8:16, :]
    b_t.start()

    def store_b(b, v):
        stb[b] = v

    weight_part(nx, rmix, store_b)
    low_cols = pl.ds(0, 128)
    sb_ = WeightScatter(stb, got1.at[1, :, :, :, low_cols], got2.at[1, :, :, low_cols], bot3, 128, usem, p)
    sb_.first()

    @pl.when(across == 0)
    def _():
        gn_sum.send_far()

    a_y.wait()
    az[p.zl] = ay[0] + ay[1] + ay[2] + ay[3]
    a_z.start()
    b_t.wait()
    bz[p.zl] = bt[0] + bt[1] + bt[2] + bt[3]
    b_z.start()
    wz_grad[...] = sz_.finish()
    a_z.wait()
    total = az[0] + az[1]
    small_out[0:8, :] = total
    high, low = split(total[5:6, :])
    pair = jnp.concatenate([high.astype(f32), low.astype(f32), jnp.zeros((14, W), f32)], axis=0).astype(bf16)
    pair = nn(pair, he[0])
    small_out[7:8, 256:384] = pair[0:1, :] + pair[1:2, :]
    b_z.wait()
    bx[p.x] = bz[0] + bz[1]
    b_x.start()
    sb_.second()
    sx_.second()
    b_x.wait()
    by[p.y] = bx[0] + bx[1] + bx[2] + bx[3]
    b_y.start()
    sb_.third()
    sx_.third()
    b_y.wait()
    small_out[8:16, :] = by[0] + by[1] + by[2] + by[3]
    wbx[me] = sb_.finish()
    e_b = Exchange(wbx, me, p.group, msem, 17)
    e_b.start()
    wx_grad[...] = sx_.finish()
    gn_sum.finish()
    for j in range(2 * NP):
        cols = slice(128 * j, 128 * j + 128)
        gate[L * (2 + j // NP):L * (3 + j // NP), 128 * (j % NP):128 * (j % NP) + 128] = gn_sum.total(slice(None), cols)
    gn_copies = [
        pltpu.make_async_copy(gate.at[pl.ds(L * (2 + h), L), :], gn_out.at[:, pl.ds(W * h, W)], hsem.at[2 + h])
        for h in range(2)
    ]
    start_all(gn_copies)
    e_b.wait()
    low = iota((48, 128), 1) < 64
    wbc_grad[:, 0:128] = jnp.where(low, wbx[0], wbx[1])
    wbc_grad[:, 128:256] = jnp.where(low, wbx[2], wbx[3])
    mine = wbx[me]
    wdt_grad[...] = jnp.where(c == 0, pltpu.roll(mine, 64, 1), mine)
    wait_all(branch_copies)
    wait_all(gn_copies)


def finish_kernel(branch, gn, x_ref, cot, norm_gain, wz, wx, wo, wbc, wdt, small,
                  block_out, input_grad, gain_grad, wz_grad, wx_grad, wbc_grad, wdt_grad, conv_x, conv_x_bias, conv_bc,
                  conv_bc_bias, dt_bias, a_log, skip, gate_norm, wo_grad):
    x = x_ref[...].astype(f32)
    block_out[...] = x + branch[...]
    inv = lax.rsqrt(jnp.mean(x * x, axis=-1, keepdims=True) + 1e-05)
    g = gn[...] * norm_gain[...].astype(f32).reshape(1, D)
    inner = jnp.mean(g * x, axis=-1, keepdims=True)
    input_grad[...] = cot[...].astype(f32) + inv * g - x * (inv * inv * inv * inner)

    @pl.when(pl.program_id(0) == 0)
    def _():
        wz_grad[...] = wz[...]
        wx_grad[...] = wx[...]
        wo_grad[...] = wo[...]
        wbc_grad[...] = wbc[...]
        wdt_grad[...] = jnp.concatenate([wdt[...], jnp.zeros((80, 128), f32)], axis=0).T[0:12, 0:48]
        conv_x[...] = small[0:4, :]
        conv_x_bias[...] = small[4:5, :].reshape(W)
        skip[...] = small[7:8, 256:268].reshape(12)
        gate_norm[...] = small[6:7, :].reshape(W)
        dt_bias[...] = small[7:8, 0:12].reshape(12)
        a_log[...] = small[7:8, 128:140].reshape(12)
        gain_grad[0:W] = small[8:9, :].reshape(W)
        gain_grad[W:D] = small[9:10, :].reshape(W)
        for k in range(3):
            conv_bc[k:k + 1, :] = small[10:11, 256 * k:256 * k + 256]
        conv_bc[3:4, :] = small[11:12, 0:256]
        conv_bc_bias[...] = small[11:12, 256:512].reshape(256)


vm = pl.BlockSpec(memory_space=pltpu.VMEM)
sm = pl.BlockSpec(memory_space=pltpu.SMEM)
hbm = pl.BlockSpec(memory_space=pl.ANY)
shape = jax.ShapeDtypeStruct
V = pltpu.VMEM


def sems(n):
    return pltpu.SemaphoreType.DMA((2, n))


def block(*args):
    rows4 = V((4, 256, D), bf16)
    scratch = dict(
        gain=V((8, D), f32), pv=V((16, W), f32), pb=V((8, 256), f32), hv=V((8, 128), f32), xg=rows4, nx=rows4, cot=rows4, wa=V((4, 4, 96, 1152), bf16), wz=V((4, 4, 96, W), bf16), wo=V((4, 4, 96, W), bf16),
        ix16=V((T, W), bf16), ixh=V((HALO, W), f32), qs=V((4, L, W), bf16), he=V((2, W, 128), bf16), csum=V((T, 128), f32),
        ibc=V((T + HALO, 256), f32), sraw=V((T, 128), f32), pre=V((T, W), f32), mixed=V((T, W), f32), yi=V((T, W), f32),
        gate=V((T, W), f32), gno=V((T, W), f32), rgate=V((4, L, W), bf16), no=V((4, L, W), bf16),
        sin=V((NC, N, W), bf16), bc16=V((T, 256), bf16), rstep=V((4, L, 128), bf16), S=V((N, W), f32),
        dpre=V((HALO, W), f32), dk=V((16, W), f32), hs=V((8, 128), f32), dbc=V((L, 256), f32),
        ssx=V((4, 8, T), f32), crx=V((4, 8, T), f32),
        near=V((2, L, D), bf16), far=V((L, D), bf16),
        stz=V((4, 4, 96, W), bf16), got1=V((2, 3, 4, 96, W), bf16), got2=V((2, 3, 96, W), bf16), got3=V((3, 48, W), bf16),
        stb=V((4, 4, 96, 128), bf16), bot3=V((48, 128), bf16),
        dsend=V((4, 4, 128, 128), bf16), drecv=V((4, 3, 128, 128), bf16), rmix=V((4, L, 128), bf16), bhalo=V((HALO, 128), f32),
        small=V((16, W), f32), ax=V((4, 8, W), f32), ay=V((4, 8, W), f32), az=V((2, 8, W), f32), bt=V((4, 8, W), f32), bz=V((2, 8, W), f32),
        bx=V((4, 8, W), f32), by=V((4, 8, W), f32),
        wbx=V((4, 48, 128), f32),
        asem=sems(21), bsem=sems(21), tsem=sems(21), xsem=sems(4), csem=sems(4), osem=sems(3), gsem=sems(3), esem=sems(6), dsem=sems(12),
        zsem=sems(13), wsem=sems(13), vsem=sems(13), usem=sems(13), msem=sems(20),
        hsem=pltpu.SemaphoreType.DMA((4,)),
    )
    return pl.pallas_call(
        mega_kernel,
        out_shape=[
            shape((256, D), f32), shape((256, D), f32), shape((48, W), f32), shape((48, W), f32), shape((48, W), f32),
            shape((48, 256), f32), shape((48, 128), f32), shape((16, W), f32),
        ],
        in_specs=[sm] + [hbm] * 5 + [vm, hbm] + [vm] * 9,
        out_specs=[hbm] * 2 + [vm] * 6,
        scratch_shapes=list(scratch.values()),
        compiler_params=pltpu.CompilerParams(collective_id=0, has_side_effects=True, vmem_limit_bytes=63 * 2**20),
        name="residual_block",
    )(*args)


def finish(*args):
    rows = pl.BlockSpec((128, D), lambda i: (i, 0))

    def whole(*dims):
        return pl.BlockSpec(dims, lambda i: (0,) * len(dims))

    outs = [(D,), (48, W), (48, W), (48, 256), (12, 48), (4, W), (W,), (4, 256), (256,), (12,), (12,), (12,), (W,), (48, W)]
    return pl.pallas_call(
        finish_kernel,
        grid=(2,),
        out_shape=[shape((256, D), f32)] * 2 + [shape(s, f32) for s in outs],
        in_specs=[rows] * 4 + [whole(D)] + [whole(48, W)] * 3 + [whole(48, 256), whole(48, 128), whole(16, W)],
        out_specs=[rows] * 2 + [whole(*s) for s in outs],
        name="finish",
    )(*args)


def per_device(hidden_in, norm_gain, w_z, w_x, w_bc, w_dt, conv_x, conv_x_bias, conv_bc, conv_bc_bias,
               dt_bias, a_log, skip_d, gate_norm, w_out, lengths, out_grad):
    branch, gn, wz, wx, wo, wbc, wdt, small = block(
        lengths, hidden_in, out_grad, w_z, w_x, w_bc, w_dt.T, w_out.T, norm_gain, conv_x, conv_x_bias, conv_bc, conv_bc_bias,
        dt_bias, a_log, skip_d, gate_norm)
    outs = list(finish(branch, gn, hidden_in, out_grad, norm_gain, wz, wx, wo, wbc, wdt, small))
    outs[6] = outs[6].T
    outs[15] = outs[15].T
    return tuple(outs)


def solution(mesh):
    rows, both = P(("dp", "tensor"), None), P("dp", "tensor")
    t = P("tensor")
    in_specs = (rows, P(), both, both, P("dp", None), both, P(None, "tensor"), t, P(), P(), t, t, t, t,
                P("tensor", "dp"), P("dp", None), rows)
    out_specs = (rows, rows, P(), both, both, P("dp", None), both, P(None, "tensor"), t, P(), P(), t, t, t, t,
                 P("tensor", "dp"))
    return jax.shard_map(per_device, mesh=mesh, in_specs=in_specs, out_specs=out_specs, check_vma=False)
```

```python
import jax
import jax.numpy as jnp
from jax import lax
from jax.experimental import pallas as pl
from jax.experimental.pallas import tpu as pltpu
from jax.sharding import PartitionSpec as P

f32=jnp.float32; bf16=jnp.bfloat16
T=1024; L=256; NC=4; D=1536; W=768; NP=6; N=128; HALO=8
HI=lax.Precision.HIGHEST
NEG=-1e30

def nn(a,b,prec=None): return lax.dot_general(a,b,(((1,),(0,)),((),())),precision=prec,preferred_element_type=f32)
def nt(a,b,prec=None): return lax.dot_general(a,b,(((1,),(1,)),((),())),precision=prec,preferred_element_type=f32)
def tn(a,b,prec=None): return lax.dot_general(a,b,(((0,),(0,)),((),())),precision=prec,preferred_element_type=f32)

def iota(shape,d): return lax.broadcasted_iota(jnp.int32,shape,d)
def seg_of(idx,ends):
    s=(idx>=ends[0]).astype(jnp.int32)
    for k in range(1,4): s=s+(idx>=ends[k]).astype(jnp.int32)
    return s
def sig(v): return 0.5*jnp.tanh(0.5*v)+0.5
def softplus(v): return jnp.maximum(v,0.0)+jnp.log1p(jnp.exp(-jnp.abs(v)))

def chunk_masks(ends,r0):
    ri=iota((L,128),0)+r0
    sg=seg_of(ri,ends)
    return sg,[None]+[(seg_of(ri-j,ends)==sg) for j in (1,2,3)]
def pair_cols(a,j,lo):
    return jnp.where(lo,a[:,2*j:2*j+1],a[:,2*j+1:2*j+2])
def split(v):
    high=v.astype(bf16)
    return high,(v-high.astype(f32)).astype(bf16)
def row_sums(tri,v,lane):
    a,rest=split(v)
    b=(v-a.astype(f32)-rest.astype(f32))
    packed=a.astype(f32)+pltpu.roll(rest.astype(f32),16,1)+pltpu.roll(b.astype(bf16).astype(f32),32,1)
    r=nn(tri.astype(bf16),packed.astype(bf16))
    return r+pltpu.roll(r,112,1)+pltpu.roll(r,96,1)
def taps(w,masks,halo):
    out=[w[halo:halo+L]]
    for q in (1,2,3):
        out.append(jnp.where(masks[q],w[halo-q:halo-q+L],0.0))
    return out
def conv_pre(ws,pv,kcols):
    s=pv[4:5,kcols]+pv[3:4,kcols]*ws[0]
    for q in (1,2,3): s=s+pv[3-q:4-q,kcols]*ws[q]
    return s

def head_steps(sraw,hv):
    dtp=sraw+hv[0:1,:]
    dt=softplus(dtp)
    return dtp,dt
def chunk_decay(ends,r0,dt,hv,ltri):
    dA=dt*hv[1:2,:]
    cs=row_sums(ltri,dA,None)
    return dA,cs
def seg_scalars(ends,r0):
    before=seg_of(r0-1,ends); last=seg_of(r0+L-1,ends)
    return before,last
def chunk_state_decays(cs,sg,before,last):
    e=jnp.where(sg==before,jnp.exp(cs),0.0)
    csl=cs[L-1:L,:]
    w=jnp.where(sg==last,jnp.exp(csl-cs),0.0)
    kd=jnp.exp(csl)*jnp.where(before==last,1.0,0.0)
    return e,w,kd

def fwd_chunk(c,ends,nx,wa,pv,pb,hv,ix16,ixh,tmp,ibc,sraw,pre,mixed,yi,sin,bc16,csum,S):
    r0=pl.multiple_of(c*L,L); rp=pl.multiple_of(c*L+HALO,8)
    rows=pl.ds(r0,L); rows_p=pl.ds(rp,L)
    n=nx[c]
    t=nn(n,wa[:,:,:,0:W].reshape(D,W))
    tmp[...]=t
    ix16[rows,:]=t.astype(bf16)
    t=nn(n,wa[:,:,:,W:].reshape(D,384))
    ibc[rows_p,:]=t[:,:256]
    sraw[rows,:]=t[:,256:]
    lane=iota((L,128),1); lo=lane<64
    sg,masks=chunk_masks(ends,r0)
    ti=iota((L,L),0); si=iota((L,L),1)
    mask=(seg_of(ti+r0,ends)==seg_of(si+r0,ends))&(ti>=si)
    ltri=(ti>=si).astype(f32)
    dtp,dt=head_steps(sraw[rows,:],hv)
    dA,cs=chunk_decay(ends,r0,dt,hv,ltri)
    csum[rows,:]=cs
    csT=cs.T
    before,last=seg_scalars(ends,r0)
    e,w,kd=chunk_state_decays(cs,sg,before,last)
    win=pl.ds(r0,L+HALO)
    bc=[]
    for k in range(2):
        cols=slice(128*k,128*k+128)
        p=conv_pre(taps(ibc[win,cols],masks,HALO),pb,cols)
        v=(p*sig(p)).astype(bf16)
        bc16[rows,cols]=v
        bc.append(v)
    B,C=bc
    BT=B.T
    sc=nt(C,B)
    for j in range(NP):
        cols=slice(128*j,128*j+128)
        p=conv_pre(taps(jnp.concatenate([ixh[:,cols],tmp[:,cols]],axis=0),masks,HALO),pv,cols)
        ixh[:,cols]=tmp[L-HALO:L,cols]
        pre[rows,cols]=p
        xc=p*sig(p)
        u=pair_cols(dt,j,lo)*xc
        ub=u.astype(bf16)
        y=None
        for q in range(2):
            h=2*j+q
            dec=jnp.exp(jnp.where(mask,cs[:,h:h+1]-csT[h:h+1,:],NEG))
            M=(sc*dec).astype(bf16)
            uq=jnp.where(lo if q==0 else ~lo,ub,jnp.zeros_like(ub))
            t=nn(M,uq)
            y=t if y is None else y+t
        yi[rows,cols]=y
        Sj=S[:,cols]
        Sb=Sj.astype(bf16)
        sin[c,:,cols]=Sb
        y=y+pair_cols(e,j,lo)*nn(C,Sb)
        mixed[rows,cols]=y+pv[6:7,cols]*xc
        uw=(u*pair_cols(w,j,lo)).astype(bf16)
        S[:,cols]=pair_cols(kd,j,lo[:1])*Sj+nn(BT,uw)

def bwd_chunk(c,ends,pv,pb,hv,ix16,ibc,sraw,pre,mixed,yi,sin,bc16,csum,gm,dS,
              qs,he,dpre,rx,dbc,rstep,dk,hs):
    r0=pl.multiple_of(c*L,L)
    rows=pl.ds(r0,L)
    lane=iota((L,128),1); lo=lane<64
    sg,masks=chunk_masks(ends,r0)
    ri=iota((L,128),0)+r0
    up=[None]+[((seg_of(ri+j,ends)==sg)&(ri+j<T)) for j in (1,2,3)]
    ti=iota((L,L),0); si=iota((L,L),1)
    maskT=(seg_of(ti+r0,ends)==seg_of(si+r0,ends))&(si>=ti)
    dtp,dt=head_steps(sraw[rows,:],hv)
    dA=dt*hv[1:2,:]
    cs=csum[rows,:]
    csT=cs.T
    before,last=seg_scalars(ends,r0)
    e,w,kd=chunk_state_decays(cs,sg,before,last)
    B=bc16[rows,0:128]; C=bc16[rows,128:256]
    CT=C.T
    scT=nt(B,C)
    acc=jnp.zeros((L,L),f32); dCin=jnp.zeros((L,N),f32); dBout=jnp.zeros((L,N),f32)
    rowq=[]
    for j in range(NP):
        cols=slice(128*j,128*j+128)
        g=gm[rows,cols]; gb=g.astype(bf16)
        p=pre[rows,cols]; s=sig(p); xc=p*s
        dtx=pair_cols(dt,j,lo)
        u=dtx*xc; ub=u.astype(bf16)
        sk=pv[6:7,cols]
        du=None
        for q in range(2):
            h=2*j+q
            dec=jnp.exp(jnp.where(maskT,csT[h:h+1,:]-cs[:,h:h+1],NEG))
            M=(scT*dec).astype(bf16)
            gq=jnp.where(lo if q==0 else ~lo,gb,jnp.zeros_like(gb))
            t=nn(M,gq)
            du=t if du is None else du+t
            acc=acc+nt(ub,gq)*dec
        dSj=dS[:,cols]; dSb=dSj.astype(bf16)
        Sb=sin[c,:,cols]
        wx_=pair_cols(w,j,lo); ex=pair_cols(e,j,lo)
        duo=wx_*nn(B,dSb)
        gef=g*ex
        ge=gef.astype(bf16); uw=(u*wx_).astype(bf16)
        dCin=dCin+nt(ge,Sb)
        dBout=dBout+nt(uw,dSb)
        yij=yi[rows,cols]
        y_in=mixed[rows,cols]-yij-sk*xc
        udo=u*duo
        qs[0,:,cols],qs[1,:,cols]=split((gb.astype(f32)*yij-ub.astype(f32)*du)+(g*y_in-udo))
        du=du+duo
        qs[2,:,cols],qs[3,:,cols]=split(xc*du)
        kdj=pair_cols(kd,j,lo[:1])
        rowq.append(jnp.sum(udo,0,keepdims=True)+jnp.sum(kdj*Sb.astype(f32)*dSj,0,keepdims=True))
        dS[:,cols]=kdj*dSj+nn(CT,ge)
        dxc=dtx*du+sk*g
        dp=dxc*(s*(1.0+p*(1.0-s)))
        v=ix16[rows,cols].astype(f32)
        dk[4:5,cols]+=jnp.sum(dp,0,keepdims=True)
        dk[5:6,cols]+=jnp.sum(g*xc,0,keepdims=True)
        dk[3:4,cols]+=jnp.sum(dp*v,0,keepdims=True)
        wd=jnp.concatenate([dp,dpre[:,cols]],axis=0)
        dpre[:,cols]=dp[0:HALO]
        dv=pv[3:4,cols]*dp
        for t_ in (1,2,3):
            later=jnp.where(up[t_],wd[t_:t_+L],0.0)
            dk[3-t_:4-t_,cols]+=jnp.sum(later*v,0,keepdims=True)
            dv=dv+pv[3-t_:4-t_,cols]*later
        rx[c,:,cols]=dv.astype(bf16)
    ab=acc.astype(bf16)
    dbc[:,0:128]=nn(ab,C)+dBout
    dbc[:,128:256]=nn(ab.T,B)+dCin
    own=lane<12
    r=nn(qs[0],he[0])+nn(qs[1],he[0])+nn(qs[2],he[1])+nn(qs[3],he[1])
    high,low=split(jnp.concatenate(rowq,axis=1))
    tails=jnp.concatenate([high.astype(f32),low.astype(f32),jnp.zeros((14,W),f32)],axis=0).astype(bf16)
    tails=nn(tails,he[0])
    dcs=r+jnp.where(iota((L,128),0)==L-1,tails[0:1,:]+tails[1:2,:],0.0)
    ddA=row_sums(si>=ti,jnp.where(own,dcs,0.0),None)
    ddt=pltpu.roll(r,96,1)+hv[1:2,:]*ddA
    hs[1:2,:]+=jnp.sum(ddA*dA,0,keepdims=True)
    dsr=jnp.where(own,ddt*sig(dtp),0.0)
    hs[0:1,:]+=jnp.sum(dsr,0,keepdims=True)
    rstep[c]=dsr.astype(bf16)
MESH = pl.DeviceIdType.MESH


def position():
    d = lax.axis_index("dp")
    t = lax.axis_index("tensor")
    return d // 8, (d // 2) % 4, d % 2, t // 2, t % 2


def device(x, y, zl, zh, c):
    return (lax.rem(x, 4) * 8 + lax.rem(y, 4) * 2 + zl, zh * 2 + c)


class Peers:
    def __init__(self):
        self.x, self.y, self.zl, self.zh, self.c = x, y, zl, zh, c = position()
        self.along_x = [device(x + k, y, zl, zh, c) for k in (1, 2, 3)]
        self.along_y = [device(x, y + k, zl, zh, c) for k in (1, 2, 3)]
        self.pair = device(x, y, 1 - zl, zh, c)
        self.far = device(x, y, zl, 1 - zh, c)
        self.near = device(x, y, zl, zh, 1 - c)
        self.cross = device(x, y, zl, 1 - zh, 1 - c)
        self.rank = zh * 2 + c
        self.group = [self.near, self.far, self.cross]
        self.all = self.along_x + self.along_y + [self.pair, self.far, self.near, self.cross]


def greet(devices):
    barrier = pltpu.get_barrier_semaphore()
    for other in devices:
        pl.semaphore_signal(barrier, inc=1, device_id=other, device_id_type=MESH)
    pl.semaphore_wait(barrier, len(devices))


def remote(src, dst, sems, k, to):
    return pltpu.make_async_remote_copy(
        src_ref=src, dst_ref=dst, send_sem=sems.at[0, k], recv_sem=sems.at[1, k], device_id=to, device_id_type=MESH
    )


def start_all(copies):
    for copy in copies:
        copy.start()


def wait_all(copies):
    for copy in copies:
        copy.wait()


class Ring:
    def __init__(self, at, mine, line, sems, first):
        plus, minus = line[0], line[2]
        before, after = lax.rem(mine + 3, 4), lax.rem(mine + 1, 4)
        own = [at(mine, 0), at(mine, 1)]
        self.own = [
            remote(own[0], own[0], sems, first, plus),
            remote(own[1], own[1], sems, first + 1, minus),
            remote(own[1], own[1], sems, first + 2, plus),
            remote(own[0], own[0], sems, first + 3, minus),
        ]
        self.onward = [
            remote(at(before, 0), at(before, 0), sems, first + 4, plus),
            remote(at(after, 1), at(after, 1), sems, first + 5, minus),
        ]

    def start(self):
        start_all(self.own)

    def forward(self):
        for k in range(2):
            self.own[k].wait()
            self.onward[k].start()

    def finish(self):
        wait_all(self.own[2:])
        wait_all(self.onward)


class WeightGather:
    def __init__(self, pieces, full, split, sems, p):
        x, y = p.x, p.y
        cols = full.shape[3]
        a, b = pl.ds(0, split), pl.ds(split, cols - split)
        mine = pl.ds(pl.multiple_of(p.zl * 48, 16), 48)
        self.mine = mine
        self.z = remote(full.at[x, y, mine, :], full.at[x, y, mine, :], sems, 0, p.pair)
        self.own = [
            pltpu.make_async_copy(piece, full.at[x, y, mine, pl.ds(at, width)], sems.at[0, 19 + k])
            for k, (piece, at, width) in enumerate(pieces)
        ]
        self.mid = []
        for k in range(3):
            ya, xb = full.at[x, y, :, a], full.at[x, y, :, b]
            self.mid.append(remote(ya, ya, sems, 1 + k, p.along_y[k]))
            self.mid.append(remote(xb, xb, sems, 4 + k, p.along_x[k]))
        self.last = [
            Ring(lambda o, h: full.at[o, pl.ds(2 * h, 2), :, a], x, p.along_x, sems, 7),
            Ring(lambda o, h: full.at[pl.ds(2 * h, 2), o, :, b], y, p.along_y, sems, 13),
        ]

    def load(self):
        start_all(self.own)

    def first(self):
        wait_all(self.own)
        self.z.start()

    def second(self):
        self.z.wait()
        start_all(self.mid)

    def third(self):
        wait_all(self.mid)
        start_all(self.last)

    def forward(self):
        for ring in self.last:
            ring.forward()

    def finish(self):
        for ring in self.last:
            ring.finish()


class WeightScatter:
    def __init__(self, part, got1, got2, got3, split, sems, p):
        x, y = p.x, p.y
        cols = got3.shape[1]
        self.part, self.got1, self.got2, self.got3, self.p = part, got1, got2, got3, p
        self.a, self.b = a, b = pl.ds(0, split), pl.ds(split, cols - split)
        mine = pl.ds(pl.multiple_of(p.zl * 48, 16), 48)
        other = pl.ds(pl.multiple_of((1 - p.zl) * 48, 16), 48)
        self.mine = mine
        self.one = []
        self.two = []
        for k in range(3):
            xk, yk = lax.rem(x + k + 1, 4), lax.rem(y + k + 1, 4)
            self.one.append(remote(part.at[xk, :, :, a], got1.at[k, :, :, a], sems, k, p.along_x[k]))
            if b.size:
                self.one.append(remote(part.at[:, yk, :, b], got1.at[k, :, :, b], sems, 3 + k, p.along_y[k]))
            self.two.append(remote(part.at[x, yk, :, a], got2.at[k, :, a], sems, 6 + k, p.along_y[k]))
            if b.size:
                self.two.append(remote(part.at[xk, y, :, b], got2.at[k, :, b], sems, 9 + k, p.along_x[k]))
        self.three = remote(part.at[x, y, other, :], got3, sems, 12, p.pair)

    def first(self):
        start_all(self.one)

    def second(self):
        wait_all(self.one)
        x, y, part, got = self.p.x, self.p.y, self.part, self.got1

        @pl.loop(0, 4)
        def _(i):
            for cut, at in ((self.a, (x, i)), (self.b, (i, y))):
                if cut.size:
                    total = part[at[0], at[1], :, cut].astype(f32)
                    for k in range(3):
                        total = total + got[k, i, :, cut].astype(f32)
                    part[at[0], at[1], :, cut] = total.astype(bf16)

        start_all(self.two)

    def third(self):
        wait_all(self.two)
        total = self.part[self.p.x, self.p.y].astype(f32)
        for k in range(3):
            total = total + self.got2[k].astype(f32)
        self.part[self.p.x, self.p.y] = total.astype(bf16)
        self.three.start()

    def finish(self):
        self.three.wait()
        return self.part[self.p.x, self.p.y, self.mine, :].astype(f32) + self.got3[...].astype(f32)


class RowGather:
    def __init__(self, own, full, sems, p):
        me, across = p.rank, (1 - p.zh) * 2 + p.c
        self.to_far = remote(own, full.at[me], sems, 0, p.far)
        self.to_near = remote(own, full.at[me], sems, 1, p.near)
        self.onward = remote(full.at[across], full.at[across], sems, 2, p.near)
        self.own = pltpu.make_async_copy(own, full.at[me], sems.at[0, 3])

    def first(self):
        self.to_far.start()
        self.to_near.start()
        self.own.start()

    def forward(self):
        self.to_far.wait()
        self.onward.start()

    def finish(self):
        self.onward.wait()


class RowScatter:
    def __init__(self, part, near, far, sems, p):
        self.part, self.near, self.far, self.p = part, near, far, p
        self.copies = [
            remote(part.at[z * 2 + 1 - p.c], near.at[k], sems, k, p.near)
            for k, z in ((0, 1 - p.zh), (1, p.zh))
        ]
        across = (1 - p.zh) * 2 + p.c
        self.across = across
        self.out = remote(part.at[across], far, sems, 2, p.far)

    def send_near(self, k):
        self.copies[k].start()

    def send_far(self):
        self.copies[0].wait_recv()

        @pl.loop(0, 4)
        def _(k):
            rows = pl.ds(pl.multiple_of(k * 64, 64), 64)
            total = self.part[self.across, rows, :].astype(f32) + self.near[0, rows, :].astype(f32)
            self.part[self.across, rows, :] = total.astype(bf16)

        self.out.start()

    def finish(self):
        self.copies[0].wait_send()
        self.copies[1].wait()
        self.out.wait()

    def total(self, rows, cols):
        return (
            self.part[self.p.rank, rows, cols].astype(f32)
            + self.near[1, rows, cols].astype(f32)
            + self.far[rows, cols].astype(f32)
        )


class Exchange:
    def __init__(self, ref, me, others, sems, first, rows=None):
        at = ref.at[me] if rows is None else ref.at[me, rows]
        self.copies = [remote(at, at, sems, first + k, to) for k, to in enumerate(others)]

    def start(self):
        start_all(self.copies)

    def wait(self):
        wait_all(self.copies)


def spread(row):
    return jnp.broadcast_to(row, (128, L)).T


def row_of(total):
    return jnp.sum(total.T, axis=0, keepdims=True)


def mega_kernel(lengths, xloc, cotloc, w_z, w_x, w_bc, w_dt, w_out, norm_gain, conv_x, conv_x_bias, conv_bc, conv_bc_bias,
                dt_bias, a_log, skip_d, gate_norm,
                branch_out, gn_out, wz_grad, wx_grad, wo_grad, wbc_grad, wdt_grad, small_out,
                gain, pv, pb, hv, xg, nx, cot, wa, wz, wo, ix16, ixh, qs, he, csum, ibc, sraw, pre, mixed, yi, gate, gno, rgate, no, sin, bc16, rstep, S,
                dpre, dk, hs, dbc, ssx, crx, near, far, stz, got1, got2, got3,
                stb, bot3, dsend, drecv, rmix, bhalo, small, ax, ay, az, bt, bz, bx, by, wbx,
                asem, bsem, tsem, xsem, csem, osem, gsem, esem, dsem, zsem, wsem, vsem, usem, msem, hsem):
    p = Peers()
    zh, c, me = p.zh, p.c, p.rank
    ga = WeightGather([(w_x, 0, W), (w_bc, W, 256)], wa, 640, asem, p)
    gz = WeightGather([(w_z, 0, W)], wz, 384, bsem, p)
    go = WeightGather([(w_out, 0, W)], wo, 384, tsem, p)
    ga.load()
    gz.load()
    go.load()
    dbc[0:128, 0:128] = jnp.zeros((128, 128), f32)
    dbc[0:12, 0:48] = w_dt[...].astype(f32)
    wa[p.x, p.y, ga.mine, W + 256:] = dbc[0:128, 0:128].T[0:48].astype(bf16)
    greet(p.all)
    gx = RowGather(xloc, xg, xsem, p)
    gc = RowGather(cotloc, cot, csem, p)
    ga.first()
    gx.first()
    gz.first()
    go.first()
    ends = [lengths[0, 0]]
    for k in range(1, 4):
        ends.append(ends[k - 1] + lengths[0, k])
    gain[0:1, :] = norm_gain[...].astype(f32).reshape(1, D)
    pv[0:4, :] = conv_x[...].astype(f32)
    pv[4:5, :] = conv_x_bias[...].astype(f32).reshape(1, W)
    pv[5:6, :] = gate_norm[...].astype(f32).reshape(1, W)
    skip = skip_d[...].reshape(1, 12)
    for j in range(NP):
        pv[6:7, 128 * j:128 * j + 128] = pair_cols(skip, j, iota((1, 128), 1) < 64)
    pb[0:4, :] = conv_bc[...].astype(f32)
    pb[4:5, :] = conv_bc_bias[...].astype(f32).reshape(1, 256)
    hv[...] = jnp.zeros((8, 128), f32)
    hv[0:1, 0:12] = dt_bias[...].reshape(1, 12)
    hv[1:2, 0:12] = -jnp.exp(a_log[...].reshape(1, 12))
    ixh[...] = jnp.zeros((HALO, W), f32)
    lane = iota((W, 128), 1)
    head = iota((W, 128), 0) // 64
    he[0] = jnp.where(lane == head, 1.0, 0.0).astype(bf16)
    he[1] = jnp.where(lane == head + 32, 1.0, 0.0).astype(bf16)
    ibc[0:HALO, :] = jnp.zeros((HALO, 256), f32)
    S[...] = jnp.zeros((N, W), f32)
    dk[...] = jnp.zeros((16, W), f32)
    hs[...] = jnp.zeros((8, 128), f32)
    small[...] = jnp.zeros((16, W), f32)
    ga.second()

    def norm_block(t):
        @pl.loop(0, 4)
        def _(k):
            rows = pl.ds(pl.multiple_of(k * 64, 64), 64)
            v = xg[t, rows, :].astype(f32)
            inv = lax.rsqrt(jnp.mean(v * v, axis=-1, keepdims=True) + 1e-05)
            nx[t, rows, :] = (v * inv * gain[0:1, :]).astype(bf16)

    gx.own.wait()
    norm_block(me)
    gx.to_near.wait()
    norm_block(zh * 2 + 1 - c)
    ga.third()
    gx.forward()
    gc.first()
    norm_block((1 - zh) * 2 + c)
    gx.finish()
    norm_block((1 - zh) * 2 + 1 - c)
    ga.forward()
    gz.second()
    ga.finish()
    gc.own.wait()
    gc.to_near.wait()
    gz.third()

    @pl.loop(0, NC)
    def _(i):
        fwd_chunk(i, ends, nx, wa, pv, pb, hv, ix16, ixh, gate.at[pl.ds(0, L), :], ibc, sraw, pre, mixed, yi, sin, bc16, csum, S)

        @pl.when(i == 0)
        def _():
            gz.forward()
            go.second()

        @pl.when(i == 1)
        def _():
            gc.forward()
            go.third()

        @pl.when(i == 2)
        def _():
            go.forward()

    gz.finish()
    gc.finish()

    e_square = Exchange(ssx, me, p.group, esem, 0)
    e_cross = Exchange(crx, me, p.group, esem, 3)

    @pl.loop(0, NC)
    def _(i):
        rows = pl.ds(pl.multiple_of(i * L, L), L)
        gate[rows, :] = nn(nx[i], wz[...].reshape(D, W))
        total = jnp.zeros((L, 128), f32)
        for j in range(NP):
            cols = slice(128 * j, 128 * j + 128)
            g = gate[rows, cols]
            gated = mixed[rows, cols] * (g * sig(g))
            total = total + gated * gated
        ssx[me, :, rows] = jnp.broadcast_to(row_of(total), (8, L))

    e_square.start()
    go.finish()

    @pl.loop(0, NC)
    def _(i):
        rows = pl.ds(pl.multiple_of(i * L, L), L)
        live = iota((L, 128), 0) + i * L < ends[3]
        for j in range(2 * NP):
            cols = slice(128 * j, 128 * j + 128)
            cot[i, :, cols] = jnp.where(live, cot[i, :, cols].astype(f32), 0.0).astype(bf16)
        gno[rows, :] = nn(cot[i], wo[...].reshape(D, W))

    e_square.wait()

    def inv_of(rows):
        square = ssx[0, 0:1, rows] + ssx[1, 0:1, rows] + ssx[2, 0:1, rows] + ssx[3, 0:1, rows]
        return lax.rsqrt(square / 3072.0 + 1e-05)

    out = RowScatter(xg, near, far, osem, p)

    @pl.loop(0, NC)
    def _(i):
        t = jnp.where(i < 2, 1 - zh, zh) * 2 + jnp.where(lax.rem(i, 2) == 0, 1 - c, c)
        rows = pl.ds(pl.multiple_of(t * L, L), L)
        inv = spread(inv_of(rows))
        cross = jnp.zeros((L, 128), f32)
        for j in range(NP):
            cols = slice(128 * j, 128 * j + 128)
            g = gate[rows, cols]
            gated = mixed[rows, cols] * (g * sig(g))
            scaled = gated * inv
            gn = pv[5:6, cols]
            go = gno[rows, cols]
            no[t, :, cols] = (scaled * gn).astype(bf16)
            dk[6:7, cols] += jnp.sum(go * scaled, 0, keepdims=True)
            cross = cross + go * gn * gated
        crx[me, :, rows] = jnp.broadcast_to(row_of(cross), (8, L))
        for k in range(2):
            xg[t, :, W * k:W * k + W] = nt(no[t], wo[2 * k:2 * k + 2].reshape(W, W)).astype(bf16)

        @pl.when(i == 0)
        def _():
            out.send_near(0)

        @pl.when(i == 2)
        def _():
            out.send_near(1)

    e_cross.start()
    out.send_far()

    def weight_part(rows_ref, grads, store):
        @pl.loop(0, 4)
        def _(b):
            left = rows_ref[:, :, pl.ds(pl.multiple_of(b * 384, 128), 384)].reshape(T, 384)
            g = grads[...].reshape(T, grads.shape[2])
            store(b, tn(left, g).astype(bf16).reshape(4, 96, grads.shape[2]))

    def store_wo(b, v):
        wo[b] = v

    weight_part(cot, no, store_wo)
    so = WeightScatter(wo, got1.at[0], got2.at[0], got3.at[0], 384, wsem, p)
    so.first()
    e_cross.wait()

    @pl.loop(0, NC)
    def _(i):
        rows = pl.ds(pl.multiple_of(i * L, L), L)
        inv_row = inv_of(rows)
        cross_row = crx[0, 0:1, rows] + crx[1, 0:1, rows] + crx[2, 0:1, rows] + crx[3, 0:1, rows]
        inv = spread(inv_row)
        back = spread(inv_row * inv_row * inv_row * cross_row / 3072.0)
        for j in range(NP):
            cols = slice(128 * j, 128 * j + 128)
            g = gate[rows, cols]
            s = sig(g)
            gs = g * s
            m = mixed[rows, cols]
            gg = inv * (gno[rows, cols] * pv[5:6, cols]) - m * gs * back
            gno[rows, cols] = gg * gs
            rgate[i, :, cols] = (gg * m * s * (1.0 + g * (1.0 - s))).astype(bf16)

    def store_z(b, v):
        stz[b] = v

    weight_part(nx, rgate, store_z)
    sz_ = WeightScatter(stz, got1.at[1], got2.at[1], got3.at[1], 384, zsem, p)
    sz_.first()

    S[...] = jnp.zeros((N, W), f32)
    dpre[...] = jnp.zeros((HALO, W), f32)

    branch_copies = [
        pltpu.make_async_copy(gate.at[pl.ds(L * h, L), :], branch_out.at[:, pl.ds(W * h, W)], hsem.at[h]) for h in range(2)
    ]

    ranks = [zh * 2 + 1 - c, (1 - zh) * 2 + c, (1 - zh) * 2 + 1 - c]
    tile = pl.ds(pl.multiple_of(zh * 128, 128), 128)
    half = (iota((L, 128), 1) // 64) == c
    bhalo[...] = jnp.zeros((HALO, 128), f32)
    for k in range(4):
        bc_tile = wa[k, :, :, pl.ds(pl.multiple_of(W + zh * 128, 128), 128)].reshape(384, 128).astype(f32)
        dt_tile = wa[k, :, :, W + 256:].reshape(384, 128).astype(f32)
        dt_tile = jnp.where(c == 0, pltpu.roll(dt_tile, 64, 1), dt_tile)
        mix = jnp.where((iota((384, 128), 1) // 64) == c, bc_tile, dt_tile)
        stb[k] = mix.astype(bf16).reshape(4, 96, 128)
    gn_sum = RowScatter(cot, near, far, gsem, p)
    across = (1 - zh) * 2 + c

    def bc_copies(q):
        return [remote(dsend.at[q, r], drecv.at[q, k], dsem, 3 * q + k, to) for k, (r, to) in enumerate(zip(ranks, p.group))]

    def pack(q):
        low = iota((128, 128), 1) < 64
        for z in range(2):
            cols = slice(128 * z, 128 * z + 128)
            top, bottom = dbc[0:128, cols], dbc[128:256, cols]
            dsend[q, 2 * z] = jnp.where(low, top, pltpu.roll(bottom, 64, 1)).astype(bf16)
            dsend[q, 2 * z + 1] = jnp.where(low, pltpu.roll(top, 64, 1), bottom).astype(bf16)

    def conv_back(q):
        r0 = pl.multiple_of(q * L, L)
        sg, masks = chunk_masks(ends, r0)
        ri = iota((L, 128), 0) + r0
        packed = dsend[q, me].astype(f32)
        for k in range(3):
            packed = packed + drecv[q, k].astype(f32)
        turned = pltpu.roll(packed, 64, 1)
        both = jnp.concatenate([jnp.where(c == 0, packed, turned), jnp.where(c == 0, turned, packed)], axis=0)
        grad = jnp.where(half, both, 0.0)
        kernel = pb[:, tile]
        ws = taps(ibc[pl.ds(r0, L + HALO), tile], masks, HALO)
        pre_bc = kernel[4:5] + kernel[3:4] * ws[0] + kernel[2:3] * ws[1] + kernel[1:2] * ws[2] + kernel[0:1] * ws[3]
        s = sig(pre_bc)
        dp = grad * (s * (1.0 + pre_bc * (1.0 - s)))
        cols = pl.ds(pl.multiple_of(256 + zh * 128, 128), 128)
        small[11:12, cols] += jnp.sum(dp, 0, keepdims=True)
        wd = jnp.concatenate([dp, bhalo[...]], axis=0)
        bhalo[...] = dp[0:HALO]
        dv = jnp.zeros((L, 128), f32)
        for t in range(4):
            later = dp
            if t:
                later = jnp.where((seg_of(ri + t, ends) == sg) & (ri + t < T), wd[t:t + L], 0.0)
            dv = dv + kernel[3 - t:4 - t] * later
            cols = pl.ds(pl.multiple_of((3 - t) % 3 * 256 + zh * 128, 128), 128)
            row = 10 if t else 11
            small[row:row + 1, cols] += jnp.sum(later * ws[0], 0, keepdims=True)
        step = rstep[q].astype(f32)
        rmix[q] = (dv + jnp.where(half, 0.0, jnp.where(c == 0, pltpu.roll(step, 64, 1), step))).astype(bf16)

    def normed_grad(q):
        for k in range(2):
            cols = slice(W * k, W * k + W)
            total = nt(rgate[q], wz[2 * k:2 * k + 2].reshape(W, W))
            total = total + nt(no[q], wa[2 * k:2 * k + 2, :, :, 0:W].reshape(W, W))
            total = total + nt(rmix[q], stb[2 * k:2 * k + 2].reshape(W, 128))
            cot[q, :, cols] = total.astype(bf16)
            weighted = jnp.sum(total * nx[q, :, cols].astype(f32), 0, keepdims=True) / gain[0:1, cols]
            small[8 + k:9 + k, :] += weighted

        @pl.when(q == (1 - zh) * 2 + 1 - c)
        def _():
            gn_sum.send_near(0)

        @pl.when(q == zh * 2 + 1 - c)
        def _():
            gn_sum.send_near(1)

    branch_copies = [
        pltpu.make_async_copy(gate.at[pl.ds(L * h, L), :], branch_out.at[:, pl.ds(W * h, W)], hsem.at[h]) for h in range(2)
    ]
    a_x = Exchange(ax, p.x, p.along_x, msem, 0)
    a_y = Exchange(ay, p.y, p.along_y, msem, 3)
    a_z = Exchange(az, p.zl, [p.pair], msem, 6)
    b_t = Exchange(bt, me, p.group, msem, 7)
    b_z = Exchange(bz, p.zl, [p.pair], msem, 10)
    b_x = Exchange(bx, p.x, p.along_x, msem, 11)
    b_y = Exchange(by, p.y, p.along_y, msem, 14)
    sx_ = WeightScatter(wo, got1.at[0], got2.at[0], got3.at[2], 384, vsem, p)

    @pl.loop(0, NC + 1)
    def _(i):
        @pl.when(i < NC)
        def _():
            q = NC - 1 - i
            bwd_chunk(q, ends, pv, pb, hv, ix16, ibc, sraw, pre, mixed, yi, sin, bc16, csum, gno,
                      S, qs, he, dpre, no, dbc, rstep, dk, hs)
            pack(q)

            @pl.when(i == 0)
            def _():
                out.finish()
                live = iota((L, 128), 0) + me * L < ends[3]
                for j in range(2 * NP):
                    cols = slice(128 * j, 128 * j + 128)
                    gate[L * (j // NP):L * (j // NP) + L, 128 * (j % NP):128 * (j % NP) + 128] = jnp.where(
                        live, out.total(slice(None), cols), 0.0)
                start_all(branch_copies)

            start_all(bc_copies(q))

            @pl.when(i == 1)
            def _():
                so.second()

            @pl.when(i == 2)
            def _():
                so.third()
                sz_.second()

            @pl.when(i == 3)
            def _():
                sz_.third()

        @pl.when(i == NC)
        def _():
            small[0:7, :] = dk[0:7, :]
            small[7:8, 0:128] = hs[0:1, :]
            small[7:8, 128:256] = hs[1:2, :]
            ax[p.x] = small[0:8, :]
            a_x.start()
            wo_grad[...] = so.finish()
            weight_part(nx, no, store_wo)
            a_x.wait()
            ay[p.y] = ax[0] + ax[1] + ax[2] + ax[3]
            a_y.start()
            sx_.first()

        @pl.when((i > 1) & (NC + 1 - i == across))
        def _():
            gn_sum.send_far()

        @pl.when(i > 0)
        def _():
            wait_all(bc_copies(NC - i))
            conv_back(NC - i)
            normed_grad(NC - i)

    bt[me] = small[8:16, :]
    b_t.start()

    def store_b(b, v):
        stb[b] = v

    weight_part(nx, rmix, store_b)
    low_cols = pl.ds(0, 128)
    sb_ = WeightScatter(stb, got1.at[1, :, :, :, low_cols], got2.at[1, :, :, low_cols], bot3, 128, usem, p)
    sb_.first()

    @pl.when(across == 0)
    def _():
        gn_sum.send_far()

    a_y.wait()
    az[p.zl] = ay[0] + ay[1] + ay[2] + ay[3]
    a_z.start()
    b_t.wait()
    bz[p.zl] = bt[0] + bt[1] + bt[2] + bt[3]
    b_z.start()
    wz_grad[...] = sz_.finish()
    a_z.wait()
    total = az[0] + az[1]
    small_out[0:8, :] = total
    high, low = split(total[5:6, :])
    pair = jnp.concatenate([high.astype(f32), low.astype(f32), jnp.zeros((14, W), f32)], axis=0).astype(bf16)
    pair = nn(pair, he[0])
    small_out[7:8, 256:384] = pair[0:1, :] + pair[1:2, :]
    b_z.wait()
    bx[p.x] = bz[0] + bz[1]
    b_x.start()
    sx_.second()
    sb_.second()
    b_x.wait()
    by[p.y] = bx[0] + bx[1] + bx[2] + bx[3]
    b_y.start()
    sb_.third()
    sx_.third()
    b_y.wait()
    small_out[8:16, :] = by[0] + by[1] + by[2] + by[3]
    wbx[me] = sb_.finish()
    e_b = Exchange(wbx, me, p.group, msem, 17)
    e_b.start()
    wx_grad[...] = sx_.finish()
    gn_sum.finish()
    for j in range(2 * NP):
        cols = slice(128 * j, 128 * j + 128)
        gate[L * (2 + j // NP):L * (3 + j // NP), 128 * (j % NP):128 * (j % NP) + 128] = gn_sum.total(slice(None), cols)
    gn_copies = [
        pltpu.make_async_copy(gate.at[pl.ds(L * (2 + h), L), :], gn_out.at[:, pl.ds(W * h, W)], hsem.at[2 + h])
        for h in range(2)
    ]
    start_all(gn_copies)
    e_b.wait()
    low = iota((48, 128), 1) < 64
    wbc_grad[:, 0:128] = jnp.where(low, wbx[0], wbx[1])
    wbc_grad[:, 128:256] = jnp.where(low, wbx[2], wbx[3])
    mine = wbx[me]
    wdt_grad[...] = jnp.where(c == 0, pltpu.roll(mine, 64, 1), mine)
    wait_all(branch_copies)
    wait_all(gn_copies)


def finish_kernel(branch, gn, x_ref, cot, norm_gain, wz, wx, wo, wbc, wdt, small,
                  block_out, input_grad, gain_grad, wz_grad, wx_grad, wbc_grad, wdt_grad, conv_x, conv_x_bias, conv_bc,
                  conv_bc_bias, dt_bias, a_log, skip, gate_norm, wo_grad):
    x = x_ref[...].astype(f32)
    block_out[...] = x + branch[...]
    inv = lax.rsqrt(jnp.mean(x * x, axis=-1, keepdims=True) + 1e-05)
    g = gn[...] * norm_gain[...].astype(f32).reshape(1, D)
    inner = jnp.mean(g * x, axis=-1, keepdims=True)
    input_grad[...] = cot[...].astype(f32) + inv * g - x * (inv * inv * inv * inner)

    @pl.when(pl.program_id(0) == 0)
    def _():
        wz_grad[...] = wz[...]
        wx_grad[...] = wx[...]
        wo_grad[...] = wo[...]
        wbc_grad[...] = wbc[...]
        wdt_grad[...] = jnp.concatenate([wdt[...], jnp.zeros((80, 128), f32)], axis=0).T[0:12, 0:48]
        conv_x[...] = small[0:4, :]
        conv_x_bias[...] = small[4:5, :].reshape(W)
        skip[...] = small[7:8, 256:268].reshape(12)
        gate_norm[...] = small[6:7, :].reshape(W)
        dt_bias[...] = small[7:8, 0:12].reshape(12)
        a_log[...] = small[7:8, 128:140].reshape(12)
        gain_grad[0:W] = small[8:9, :].reshape(W)
        gain_grad[W:D] = small[9:10, :].reshape(W)
        for k in range(3):
            conv_bc[k:k + 1, :] = small[10:11, 256 * k:256 * k + 256]
        conv_bc[3:4, :] = small[11:12, 0:256]
        conv_bc_bias[...] = small[11:12, 256:512].reshape(256)


vm = pl.BlockSpec(memory_space=pltpu.VMEM)
sm = pl.BlockSpec(memory_space=pltpu.SMEM)
hbm = pl.BlockSpec(memory_space=pl.ANY)
shape = jax.ShapeDtypeStruct
V = pltpu.VMEM


def sems(n):
    return pltpu.SemaphoreType.DMA((2, n))


def block(*args):
    rows4 = V((4, 256, D), bf16)
    scratch = dict(
        gain=V((8, D), f32), pv=V((16, W), f32), pb=V((8, 256), f32), hv=V((8, 128), f32), xg=rows4, nx=rows4, cot=rows4, wa=V((4, 4, 96, 1152), bf16), wz=V((4, 4, 96, W), bf16), wo=V((4, 4, 96, W), bf16),
        ix16=V((T, W), bf16), ixh=V((HALO, W), f32), qs=V((4, L, W), bf16), he=V((2, W, 128), bf16), csum=V((T, 128), f32),
        ibc=V((T + HALO, 256), f32), sraw=V((T, 128), f32), pre=V((T, W), f32), mixed=V((T, W), f32), yi=V((T, W), f32),
        gate=V((T, W), f32), gno=V((T, W), f32), rgate=V((4, L, W), bf16), no=V((4, L, W), bf16),
        sin=V((NC, N, W), bf16), bc16=V((T, 256), bf16), rstep=V((4, L, 128), bf16), S=V((N, W), f32),
        dpre=V((HALO, W), f32), dk=V((16, W), f32), hs=V((8, 128), f32), dbc=V((L, 256), f32),
        ssx=V((4, 8, T), f32), crx=V((4, 8, T), f32),
        near=V((2, L, D), bf16), far=V((L, D), bf16),
        stz=V((4, 4, 96, W), bf16), got1=V((2, 3, 4, 96, W), bf16), got2=V((2, 3, 96, W), bf16), got3=V((3, 48, W), bf16),
        stb=V((4, 4, 96, 128), bf16), bot3=V((48, 128), bf16),
        dsend=V((4, 4, 128, 128), bf16), drecv=V((4, 3, 128, 128), bf16), rmix=V((4, L, 128), bf16), bhalo=V((HALO, 128), f32),
        small=V((16, W), f32), ax=V((4, 8, W), f32), ay=V((4, 8, W), f32), az=V((2, 8, W), f32), bt=V((4, 8, W), f32), bz=V((2, 8, W), f32),
        bx=V((4, 8, W), f32), by=V((4, 8, W), f32),
        wbx=V((4, 48, 128), f32),
        asem=sems(21), bsem=sems(21), tsem=sems(21), xsem=sems(4), csem=sems(4), osem=sems(3), gsem=sems(3), esem=sems(6), dsem=sems(12),
        zsem=sems(13), wsem=sems(13), vsem=sems(13), usem=sems(13), msem=sems(20),
        hsem=pltpu.SemaphoreType.DMA((4,)),
    )
    return pl.pallas_call(
        mega_kernel,
        out_shape=[
            shape((256, D), f32), shape((256, D), f32), shape((48, W), f32), shape((48, W), f32), shape((48, W), f32),
            shape((48, 256), f32), shape((48, 128), f32), shape((16, W), f32),
        ],
        in_specs=[sm] + [hbm] * 5 + [vm, hbm] + [vm] * 9,
        out_specs=[hbm] * 2 + [vm] * 6,
        scratch_shapes=list(scratch.values()),
        compiler_params=pltpu.CompilerParams(collective_id=0, has_side_effects=True, vmem_limit_bytes=63 * 2**20),
        name="residual_block",
    )(*args)


def finish(*args):
    rows = pl.BlockSpec((128, D), lambda i: (i, 0))

    def whole(*dims):
        return pl.BlockSpec(dims, lambda i: (0,) * len(dims))

    outs = [(D,), (48, W), (48, W), (48, 256), (12, 48), (4, W), (W,), (4, 256), (256,), (12,), (12,), (12,), (W,), (48, W)]
    return pl.pallas_call(
        finish_kernel,
        grid=(2,),
        out_shape=[shape((256, D), f32)] * 2 + [shape(s, f32) for s in outs],
        in_specs=[rows] * 4 + [whole(D)] + [whole(48, W)] * 3 + [whole(48, 256), whole(48, 128), whole(16, W)],
        out_specs=[rows] * 2 + [whole(*s) for s in outs],
        name="finish",
    )(*args)


def per_device(hidden_in, norm_gain, w_z, w_x, w_bc, w_dt, conv_x, conv_x_bias, conv_bc, conv_bc_bias,
               dt_bias, a_log, skip_d, gate_norm, w_out, lengths, out_grad):
    branch, gn, wz, wx, wo, wbc, wdt, small = block(
        lengths, hidden_in, out_grad, w_z, w_x, w_bc, w_dt.T, w_out.T, norm_gain, conv_x, conv_x_bias, conv_bc, conv_bc_bias,
        dt_bias, a_log, skip_d, gate_norm)
    outs = list(finish(branch, gn, hidden_in, out_grad, norm_gain, wz, wx, wo, wbc, wdt, small))
    outs[6] = outs[6].T
    outs[15] = outs[15].T
    return tuple(outs)


def solution(mesh):
    rows, both = P(("dp", "tensor"), None), P("dp", "tensor")
    t = P("tensor")
    in_specs = (rows, P(), both, both, P("dp", None), both, P(None, "tensor"), t, P(), P(), t, t, t, t,
                P("tensor", "dp"), P("dp", None), rows)
    out_specs = (rows, rows, P(), both, both, P("dp", None), both, P(None, "tensor"), t, P(), P(), t, t, t, t,
                 P("tensor", "dp"))
    return jax.shard_map(per_device, mesh=mesh, in_specs=in_specs, out_specs=out_specs, check_vma=False)
```
